256 devices in a mesh: seg: 32 (over z, x), head: 8 (over y, core).
Axes of the slice: x: 4, y: 4, z: 8, core: 2. Of those that a mesh axis runs over, the one named last changes fastest.
Arguments:
- queries: bfloat16 [16384, 8192], P('seg', 'head'), may hold values from -80 to 80
- keys: bfloat16 [16384, 1024], P('seg', 'head'), may hold values from -5 to 5
- values: bfloat16 [16384, 1024], P('seg', 'head'), may hold values from -5 to 5
- out_grad: bfloat16 [16384, 8192], P('seg', 'head'), may hold values from -0.29882812 to 0.29882812
- reward_weight: float32 [8192], P('head'), may hold values from -0.3 to 0.3
- parent: int32 [32], replicated, may hold values from -1 to 30, as said below
- step_ends: int32 [32, 4], P('seg'), may hold values from 0 to 511, as said below
- target: float32 [32, 4], replicated, may hold values from -4 to 4
Outputs:
- attended: bfloat16 [16384, 8192], P('seg', 'head')
- scores: float32 [32, 4], P('seg')
- q_grad: bfloat16 [16384, 8192], P('seg', 'head')
- k_grad: bfloat16 [16384, 1024], P('seg', 'head')
- v_grad: bfloat16 [16384, 1024], P('seg', 'head')
The draws below stay inside these ranges and needn't reach their ends.
Inputs may be any that keep to these rules, and one draw needn't show every extreme that they name: Segments stand in depth-first pre-order: every subtree occupies consecutive segments and parent[i] < i; segment 0 is the only root (-1); segment 32 // 2 has segment 0 as an ancestor; segment 32 - 1 is a child of segment 32 - 2; every segment has at most 2 ancestors and some segment has exactly that many. `step_ends`: each row rises strictly and ends with 511.
All inputs are finite; a program needn't handle non-finite values.
Results may differ from the reference program's by a relative error of at most 0.018.
Values may be sent and summed in bfloat16 or wider, within the bound.
A program may use at most 192 MiB of HBM per device.

```python
import math
import jax
import jax.numpy as jnp
from jax import lax

HEADS = 64
KV_HEADS = 8
HEAD_DIM = 128
SEG_TOK = 512
MAXD = 3
STEPS = 4
GROUP = 8
SEGS = 32
TOKENS = 16384


def shared_base(key):
    return jnp.clip(jax.random.normal(key, (TOKENS, KV_HEADS * HEAD_DIM), jnp.float32), -4.0, 4.0)


def draw_keys(key, part):
    base = shared_base(key)
    return base.astype(jnp.bfloat16)


def draw_queries(key, part):
    key = jax.random.fold_in(key, 7)
    return jnp.clip(jax.random.normal(key, (TOKENS, HEADS * HEAD_DIM), jnp.float32), -4.0, 4.0).astype(jnp.bfloat16)


def draw_parent(key, part):
    key = jax.random.fold_in(key, 11)
    random_picks = jax.random.randint(key, (SEGS,), 0, 1 << 20)
    seg_order = jnp.arange(SEGS, dtype=jnp.int32)
    middle = SEGS // 2

    def advance(state, element):
        depth_prev, latest = state
        seg_index, pick_value = element
        depth_room = jnp.minimum(depth_prev + 1, MAXD - 1)
        drawn = 1 + pick_value % jnp.maximum(depth_room, 1)
        drawn = jnp.where(seg_index == middle, 1, drawn)
        drawn = jnp.where(seg_index == SEGS - 2, 1, drawn)
        drawn = jnp.where(seg_index == SEGS - 1, 2, drawn)
        tree_depth = jnp.where(seg_index < MAXD, seg_index, drawn)
        parent_id = jnp.where(tree_depth > 0, latest[jnp.maximum(tree_depth - 1, 0)], -1)
        latest = latest.at[tree_depth].set(seg_index)
        return ((tree_depth, latest), parent_id)
    start_state = (jnp.int32(-1), jnp.full((MAXD,), -1, jnp.int32))
    _, parent = lax.scan(advance, start_state, (seg_order, random_picks))
    return parent.astype(jnp.int32)


def draw_step_ends(key, part):
    key = jax.random.fold_in(key, 23)
    row_keys = jax.random.split(key, SEGS)

    def one_row(row_key):
        chosen = jax.random.permutation(row_key, SEG_TOK - 1)[:STEPS - 1]
        return jnp.concatenate([jnp.sort(chosen), jnp.full((1,), SEG_TOK - 1, chosen.dtype)])
    return jax.vmap(one_row)(row_keys).astype(jnp.int32)


def level_of(rng, shape, shards, least, top_value):
    gain, own = 1.0, jax.random.fold_in(rng, 6)
    for axis_at, parts in shards:
        steps = jnp.exp(jax.random.uniform(jax.random.fold_in(own, axis_at), (parts,), jnp.float32, least / len(shards), top_value / len(shards)))
        gain = gain * jnp.repeat(steps, shape[axis_at] // parts).reshape([-1 if axis == axis_at else 1 for axis in range(len(shape))])
    return gain


def gaussian(rng, shape, scale, most, shards=(), kind=jnp.bfloat16):
    entries = scale * jax.random.normal(rng, shape, jnp.float32)
    if shards:
        entries = entries * level_of(rng, shape, shards, -0.22, 0.18)
    return jnp.clip(entries, -most, most).astype(kind)


def setup_inputs(seed: int = 0) -> dict:
    seeds = jax.random.split(jax.random.key(seed), 9)
    return {
        "queries": draw_queries(jax.random.fold_in(seeds[8], 71), 0),
        "keys": draw_keys(jax.random.fold_in(seeds[8], 71), 0),
        "values": gaussian(seeds[2], (TOKENS, KV_HEADS * HEAD_DIM), 1.0, 5.0, ((0, 32), (1, 8))),
        "out_grad": gaussian(seeds[3], (TOKENS, HEADS * HEAD_DIM), 0.05, 0.29882812, ((0, 32), (1, 8))),
        "reward_weight": gaussian(seeds[4], (HEADS * HEAD_DIM,), 0.05, 0.3, ((0, 8),), jnp.float32),
        "parent": draw_parent(jax.random.fold_in(seeds[8], 71), 0),
        "step_ends": draw_step_ends(jax.random.fold_in(seeds[8], 71), 0),
        "target": gaussian(seeds[7], (SEGS, STEPS), 1.0, 4.0, (), jnp.float32),
    }


def ancestry(parent, segment, slot_count):
    lineage = []
    current = parent[segment]
    for slot_id in range(slot_count):
        lineage.append(current)
        current = jnp.where(current >= 0, parent[jnp.maximum(current, 0)], -1)
    lineage = jnp.stack(lineage)
    tree_depth = jnp.sum((lineage >= 0).astype(jnp.int32))
    level_ids = jnp.arange(slot_count, dtype=jnp.int32)
    reach = jnp.clip(tree_depth - 1 - level_ids, 0, slot_count - 1)
    owners = jnp.where(level_ids < tree_depth, lineage[reach], -1)
    return (owners.astype(jnp.int32), tree_depth)

def key_mask(tree_depth, slot_count, tok_rows):
    level_ids = jnp.arange(slot_count, dtype=jnp.int32)
    far_keys = jnp.repeat(level_ids < tree_depth, tok_rows)
    far_keys = jnp.broadcast_to(far_keys[None, :], (tok_rows, slot_count * tok_rows))
    positions = jnp.arange(tok_rows, dtype=jnp.int32)
    own_keys = positions[None, :] <= positions[:, None]
    return jnp.concatenate([far_keys, own_keys], axis=1)

def standardize(rewards, parent):
    segments = rewards.shape[0]
    parent_hot = (parent[:, None] == jnp.arange(segments, dtype=jnp.int32)[None, :]).astype(rewards.dtype)
    before = jnp.dot(parent_hot, rewards[:, -1], precision=lax.Precision.HIGHEST)
    previous = jnp.concatenate([before[:, None], rewards[:, :-1]], axis=1)
    margin = rewards - previous
    siblings = (parent[:, None] == parent[None, :]).astype(rewards.dtype)
    group_count = lax.optimization_barrier(jnp.sum(siblings, axis=1))[:, None]
    group_mean = jnp.dot(siblings, margin, precision=lax.Precision.HIGHEST) / group_count
    centered = margin - group_mean
    spread = jnp.dot(siblings, centered * centered, precision=lax.Precision.HIGHEST) / group_count
    return centered * lax.rsqrt(jnp.maximum(spread, 0.25))

def context(segment, queries, keys, values, parent):
    slot_count = MAXD - 1
    owners, tree_depth = ancestry(parent, segment, slot_count)
    key_rows = []
    value_rows = []
    for slot_id in range(slot_count):
        start_row = (jnp.maximum(owners[slot_id], 0) * SEG_TOK).astype(jnp.int32)
        key_rows.append(lax.dynamic_slice_in_dim(keys, start_row, SEG_TOK, 0))
        value_rows.append(lax.dynamic_slice_in_dim(values, start_row, SEG_TOK, 0))
    start_row = (segment * SEG_TOK).astype(jnp.int32)
    key_rows.append(lax.dynamic_slice_in_dim(keys, start_row, SEG_TOK, 0))
    value_rows.append(lax.dynamic_slice_in_dim(values, start_row, SEG_TOK, 0))
    key_all = jnp.concatenate(key_rows, axis=0).reshape(-1, KV_HEADS, HEAD_DIM)
    value_all = jnp.concatenate(value_rows, axis=0).reshape(-1, KV_HEADS, HEAD_DIM)
    query_seg = lax.dynamic_slice_in_dim(queries, start_row, SEG_TOK, 0).reshape(SEG_TOK, KV_HEADS, GROUP, HEAD_DIM)
    allowed = key_mask(tree_depth, slot_count, SEG_TOK)
    return (owners, query_seg, key_all, value_all, allowed)

def probabilities(query_seg, key_all, allowed):
    score_scale = 1.0 / math.sqrt(HEAD_DIM)
    logits = jnp.einsum('tkgd,mkd->kgtm', query_seg.astype(jnp.float32), key_all.astype(jnp.float32)) * score_scale
    logits = jnp.where(allowed, logits, -jnp.inf)
    row_top = lax.optimization_barrier(jnp.max(logits, axis=-1, keepdims=True))
    weights = jnp.exp(logits - row_top)
    return weights / lax.optimization_barrier(jnp.sum(weights, axis=-1, keepdims=True))

def reference(queries, keys, values, out_grad, reward_weight, parent, step_ends, target):
    score_scale = 1.0 / math.sqrt(HEAD_DIM)
    kv_width = KV_HEADS * HEAD_DIM
    seg_ids = jnp.arange(SEGS, dtype=jnp.int32)

    def attend(segment):
        owners, query_seg, key_all, value_all, allowed = context(segment, queries, keys, values, parent)
        prob_full = probabilities(query_seg, key_all, allowed)
        prob_bf = lax.optimization_barrier(prob_full.astype(jnp.bfloat16)).astype(jnp.float32)
        output = jnp.einsum('kgtm,mkd->tkgd', prob_bf, value_all.astype(jnp.float32))
        return output.astype(jnp.bfloat16).reshape(SEG_TOK, HEADS * HEAD_DIM)
    attended = lax.map(attend, seg_ids).reshape(TOKENS, HEADS * HEAD_DIM)
    picked = jnp.take_along_axis(attended.reshape(SEGS, SEG_TOK, -1), step_ends[:, :, None].astype(jnp.int32), axis=1)
    rewards = jnp.einsum('ste,e->st', picked.astype(jnp.float32), reward_weight, precision=lax.Precision.HIGHEST)
    scores, pullback = jax.vjp(lambda reward_in: standardize(reward_in, parent), rewards)
    reward_grad = pullback(target)[0]

    def backward(totals, segment):
        key_total, value_total = totals
        owners, query_seg, key_all, value_all, allowed = context(segment, queries, keys, values, parent)
        prob_full = probabilities(query_seg, key_all, allowed)
        prob_bf = lax.optimization_barrier(prob_full.astype(jnp.bfloat16)).astype(jnp.float32)
        start_row = (segment * SEG_TOK).astype(jnp.int32)
        tok_ids = jnp.arange(SEG_TOK, dtype=jnp.int32)
        picker = (step_ends[segment][:, None] == tok_ids[None, :]).astype(jnp.float32)
        step_grad = jnp.dot(picker.T, reward_grad[segment], precision=lax.Precision.HIGHEST)
        out_seg = lax.dynamic_slice_in_dim(out_grad, start_row, SEG_TOK, 0).astype(jnp.float32)
        grad_out = (out_seg + step_grad[:, None] * reward_weight[None, :]).astype(jnp.bfloat16)
        grad_four = lax.optimization_barrier(grad_out).astype(jnp.float32).reshape(SEG_TOK, KV_HEADS, GROUP, HEAD_DIM)
        att_four = lax.dynamic_slice_in_dim(attended, start_row, SEG_TOK, 0).astype(jnp.float32).reshape(SEG_TOK, KV_HEADS, GROUP, HEAD_DIM)
        row_delta = lax.optimization_barrier(jnp.sum(grad_four * att_four, axis=-1)).transpose(1, 2, 0)
        dprob = jnp.einsum('tkgd,mkd->kgtm', grad_four, value_all.astype(jnp.float32))
        dlogit = (prob_full * (dprob - row_delta[..., None])).astype(jnp.bfloat16)
        dlogit = lax.optimization_barrier(dlogit).astype(jnp.float32)
        query_grad = (jnp.einsum('kgtm,mkd->tkgd', dlogit, key_all.astype(jnp.float32)) * score_scale).astype(jnp.bfloat16)
        key_part = jnp.einsum('kgtm,tkgd->mkd', dlogit, query_seg.astype(jnp.float32)) * score_scale
        value_part = jnp.einsum('kgtm,tkgd->mkd', prob_bf, grad_four)
        key_part = key_part.reshape(MAXD, SEG_TOK, kv_width)
        value_part = value_part.reshape(MAXD, SEG_TOK, kv_width)
        for slot_id in range(MAXD - 1):
            target_row = jnp.maximum(owners[slot_id], 0).astype(jnp.int32)
            alive = owners[slot_id] >= 0
            key_total = key_total.at[target_row].add(jnp.where(alive, key_part[slot_id], 0.0))
            value_total = value_total.at[target_row].add(jnp.where(alive, value_part[slot_id], 0.0))
        key_total = key_total.at[segment].add(key_part[MAXD - 1])
        value_total = value_total.at[segment].add(value_part[MAXD - 1])
        return ((key_total, value_total), query_grad.reshape(SEG_TOK, HEADS * HEAD_DIM))
    empty = jnp.zeros((SEGS, SEG_TOK, kv_width), jnp.float32)
    (key_total, value_total), query_grads = lax.scan(backward, (empty, empty), seg_ids)
    q_grad = query_grads.reshape(TOKENS, HEADS * HEAD_DIM)
    k_grad = key_total.reshape(TOKENS, kv_width).astype(jnp.bfloat16)
    v_grad = value_total.reshape(TOKENS, kv_width).astype(jnp.bfloat16)
    return (attended, scores, q_grad, k_grad, v_grad)
```

```python
import math

import jax
import jax.numpy as jnp
from jax import lax
from jax.experimental import pallas as pl
from jax.experimental.pallas import tpu as pltpu
from jax.sharding import PartitionSpec as P

HEAD = 128
ROWS = 512
NH = 8
COLS = 4
ZS = 8
QUART = ROWS // COLS
HALF = ROWS // 2
SCALE = 1.0 / math.sqrt(HEAD)
C2 = SCALE * math.log2(math.e)
BF = jnp.bfloat16
F32 = jnp.float32
NEG = float("-inf")
MESH = pl.DeviceIdType.MESH
OWN, ROOT, PAR = 0, 1, 2


def nn(a, b):
    return jnp.dot(a, b, preferred_element_type=F32)


def nt(a, b):
    return lax.dot_general(a, b, (((1,), (1,)), ((), ())), preferred_element_type=F32)


def hot(cond):
    return jnp.where(cond, 1.0, 0.0).astype(F32)


def exact(a, b):
    return jnp.dot(a, b, preferred_element_type=F32, precision=lax.Precision.HIGHEST)


def standardize(rew, tgt, par_ref):
    segs = COLS * ZS
    lane = lax.broadcasted_iota(jnp.int32, (HEAD, HEAD), 1)
    sub = lax.broadcasted_iota(jnp.int32, (HEAD, HEAD), 0)
    prow = jnp.full((HEAD, HEAD), -2.0, F32)
    for s in range(segs):
        prow = jnp.where(lane == s, par_ref[s].astype(F32), prow)
    pcol = prow.T
    inside = (lane < segs) & (sub < segs)
    sib = jnp.where(inside & (prow == pcol), 1.0, 0.0)
    up = jnp.where(inside & (prow == sub.astype(F32)), 1.0, 0.0)
    down = up.T
    cnt = jnp.maximum(jnp.sum(sib, axis=0, keepdims=True), 1.0)
    row = lax.broadcasted_iota(jnp.int32, (8, HEAD), 0)
    used = row < 4
    before = exact(rew, up)
    shifted = jnp.concatenate([before[3:4], rew[0:7]], axis=0)
    margin = jnp.where(used, rew - shifted, 0.0)
    mean = exact(margin, sib) / cnt
    cen = margin - mean
    var = exact(cen * cen, sib) / cnt
    floor = jnp.maximum(var, 0.25)
    inv = lax.rsqrt(floor)
    scores = cen * inv
    slope = jnp.where(var > 0.25, 1.0, jnp.where(var == 0.25, 0.5, 0.0))
    dvar = tgt * cen * (-0.5) * inv / floor * slope
    dcen = tgt * inv + 2.0 * cen * exact(dvar / cnt, sib)
    dmar = jnp.where(used, dcen - exact(dcen / cnt, sib), 0.0)
    back = exact(dmar, down)
    later = jnp.concatenate([dmar[1:8], dmar[0:1]], axis=0)
    later = jnp.where(row < 3, later, jnp.where(row == 3, back[0:1], 0.0))
    return scores, dmar - later


def kernel(
    q_ref, k_ref, v_ref, g_ref, w_ref, par_ref, ends_ref, tgt_ref,
    att_ref, sc_ref, dq_ref, dk_ref, dv_ref,
    kvo, kvr, kvp, vt, kt, pbuf, oacc, mrun, lrun, mblk, got, dl, fs, dqt, dka, dva,
    rowbuf, zbuf, rootq, psend, hrx, rrow, rall, rsend, stepg,
    grs, gps, grx, gpx, cbuf, rrs, rrx, rsumq, fsend, frx,
    ssem, rsem,
):
    me = lax.axis_index("seg")
    hd = lax.axis_index("head")
    z = me // COLS
    x = me % COLS
    xs = [(x + d) % COLS for d in range(COLS)]
    xdev = [z * COLS + c for c in xs]
    zdev = [((z + d) % ZS) * COLS + x for d in range(ZS)]
    count = [0]

    def ids(n):
        count[0] += n
        return count[0] - n

    def seg_copy(src, dst, i, seg):
        return pltpu.make_async_remote_copy(
            src_ref=src, dst_ref=dst, send_sem=ssem.at[i], recv_sem=rsem.at[i],
            device_id=(seg, hd), device_id_type=MESH,
        )

    def head_copy(src, dst, i, head):
        return pltpu.make_async_remote_copy(
            src_ref=src, dst_ref=dst, send_sem=ssem.at[i], recv_sem=rsem.at[i],
            device_id=(me, head), device_id_type=MESH,
        )

    sent = []

    def hs(h):
        return pl.ds(pl.multiple_of(h * HEAD, HEAD), HEAD)

    def quarter(c):
        return pl.ds(pl.multiple_of(c * QUART, QUART), QUART)

    def loop(lo, hi, fn):
        def step(h, carry):
            fn(h)
            return carry
        lax.fori_loop(lo, hi, step, 0)

    barrier = pltpu.get_barrier_semaphore()
    for d in range(1, COLS):
        pl.semaphore_signal(barrier, inc=1, device_id=(xdev[d], hd), device_id_type=MESH)
    for d in range(1, ZS):
        pl.semaphore_signal(barrier, inc=1, device_id=(zdev[d], hd), device_id_type=MESH)
    for d in range(1, NH):
        pl.semaphore_signal(barrier, inc=1, device_id=(me, (hd + d) % NH), device_id_type=MESH)
    kvo[:, 0:HEAD] = k_ref[...]
    kvo[:, HEAD:] = v_ref[...]
    pl.semaphore_wait(barrier, COLS - 1 + ZS - 1 + NH - 1)

    base = ids(3)
    first = []
    for d in range(1, COLS):
        c = seg_copy(kvo.at[quarter(xs[d]), :], rowbuf.at[x], base + d - 1, xdev[d])
        c.start()
        first.append(c)
    sent += first
    rowbuf[x] = kvo[quarter(x), :]

    lowest = lax.broadcasted_iota(jnp.int32, (HALF, HALF), 0)
    diag = lowest <= lax.broadcasted_iota(jnp.int32, (HALF, HALF), 1)

    def flip(b, kv):
        kt[b] = kv[:, 0:HEAD].T
        vt[b, 0:HEAD, :] = kv[:, HEAD:].T
        vt[b, HEAD:, :] = jnp.ones((16, ROWS), BF)

    def own_fwd(h):
        q = q_ref[:, hs(h)]
        qa, qb = q[0:HALF], q[HALF:]
        ka, kb = kvo[0:HALF, 0:HEAD], kvo[HALF:, 0:HEAD]
        s1 = jnp.where(diag, nt(ka, qa), NEG)
        s2 = nt(ka, qb)
        s3 = jnp.where(diag, nt(kb, qb), NEG)
        m1 = jnp.max(s1, axis=0, keepdims=True)
        m2 = jnp.maximum(jnp.max(s2, axis=0, keepdims=True), jnp.max(s3, axis=0, keepdims=True))
        p1 = jnp.exp2((s1 - m1) * C2).astype(BF)
        p2 = jnp.exp2((s2 - m2) * C2).astype(BF)
        p3 = jnp.exp2((s3 - m2) * C2).astype(BF)
        pbuf[OWN, h, 0:HALF, 0:HALF] = p1
        pbuf[OWN, h, 0:HALF, HALF:] = p2
        pbuf[OWN, h, HALF:, HALF:] = p3
        o1 = nn(vt[OWN, :, 0:HALF], p1)
        o2 = nn(vt[OWN, :, 0:HALF], p2) + nn(vt[OWN, :, HALF:], p3)
        oacc[h, :, 0:HALF] = o1[0:HEAD]
        oacc[h, :, HALF:] = o2[0:HEAD]
        lrun[h, :, 0:HALF] = o1[HEAD:HEAD + 1]
        lrun[h, :, HALF:] = o2[HEAD:HEAD + 1]
        mrun[h, :, 0:HALF] = m1
        mrun[h, :, HALF:] = m2
        mblk[OWN, h, :, 0:HALF] = m1
        mblk[OWN, h, :, HALF:] = m2

    my_par = par_ref[me]
    bias = {
        ROOT: jnp.where(my_par >= 0, 0.0, NEG).astype(F32),
        PAR: jnp.where(my_par > 0, 0.0, NEG).astype(F32),
    }

    def far_fwd(b, kv):
        def run(h):
            s = nt(kv[:, 0:HEAD], q_ref[:, hs(h)])
            m = jnp.max(s, axis=0, keepdims=True)
            p = jnp.exp2((s - m) * C2).astype(BF)
            pbuf[b, h] = p
            o = nn(vt[b], p)
            top = m + bias[b]
            old = mrun[h]
            new = jnp.maximum(old, top)
            a = jnp.exp2((old - new) * C2)
            e = jnp.exp2((top - new) * C2)
            oacc[h] = oacc[h] * a + o[0:HEAD] * e
            lrun[h] = lrun[h] * a + o[HEAD:HEAD + 1] * e
            mrun[h] = new
            mblk[b, h] = top
        return run

    def ring(buf, hooks, extra=None):
        base = ids(ZS - 1)
        for hop in range(ZS // 2):
            up = seg_copy(buf.at[(z + ZS - hop) % ZS], buf.at[(z + ZS - hop) % ZS], base + hop, zdev[1])
            up.start()
            down = None
            if hop < ZS // 2 - 1:
                down = seg_copy(buf.at[(z + hop) % ZS], buf.at[(z + hop) % ZS], base + ZS // 2 + hop, zdev[ZS - 1])
                down.start()
            if extra is not None:
                extra(hop)
            hooks[hop]()
            up.wait_recv()
            sent.append(up)
            if down is not None:
                down.wait_recv()
                sent.append(down)

    flip(OWN, kvo)
    loop(0, 1, own_fwd)
    for c in first:
        c.wait_recv()

    last = jnp.int32(0)
    for t in range(COLS):
        last = jnp.where(par_ref[z * COLS + t] == 0, t, last)
    zbuf[z] = rowbuf[last]
    for t in range(COLS):
        zbuf[ZS + t] = rowbuf[t]

    @pl.when(z == 0)
    def _():
        rootq[...] = rowbuf[0]

    rbase = ids(2)

    def root_copy(way):
        return seg_copy(rootq, rootq, rbase + way, zdev[1] if way == 0 else zdev[ZS - 1])

    def root_ride(hop):
        @pl.when(z == hop)
        def _():
            if hop > 0:
                root_copy(0).wait_recv()
            root_copy(0).start()
        if hop < ZS // 2 - 1:
            @pl.when(z == (ZS - hop) % ZS)
            def _():
                if hop > 0:
                    root_copy(1).wait_recv()
                root_copy(1).start()

    ring(zbuf, [lambda i=i: loop(1 + i, 2 + i, own_fwd) for i in range(4)], root_ride)

    @pl.when(z == ZS // 2)
    def _():
        root_copy(0).wait_recv()

    @pl.when(z == ZS // 2 + 1)
    def _():
        root_copy(1).wait_recv()

    base = ids(6)
    third = []
    for d in range(1, COLS):
        c = seg_copy(rootq, kvr.at[quarter(x), :], base + d - 1, xdev[d])
        c.start()
        third.append(c)
    kvr[quarter(x), :] = rootq[...]

    def place(c):
        p = jnp.maximum(par_ref[z * COLS + c], 0)
        return jnp.where(p // COLS == z, ZS + p % COLS, p // COLS)

    for d in range(1, COLS):
        psend[d - 1] = zbuf[place(xs[d])]
        c = seg_copy(psend.at[d - 1], kvp.at[quarter(x), :], base + 2 + d, xdev[d])
        c.start()
        third.append(c)
    kvp[quarter(x), :] = zbuf[place(x)]
    sent += third

    loop(5, 8, own_fwd)
    for c in third[0:3]:
        c.wait_recv()
    flip(ROOT, kvr)
    loop(0, 4, far_fwd(ROOT, kvr))
    for c in third[3:]:
        c.wait_recv()
    flip(PAR, kvp)

    lane = lax.broadcasted_iota(jnp.int32, (8, ROWS), 1)
    sub = lax.broadcasted_iota(jnp.int32, (8, ROWS), 0)
    ends = [ends_ref[0, t] for t in range(4)]
    pick = jnp.zeros((8, ROWS), F32)
    for t in range(4):
        pick = jnp.where((sub == t) & (lane == ends[t]), 1.0, pick)
    picked = nn(pick.astype(BF), q_ref[...])
    qs = jnp.concatenate([picked[:, h * HEAD:(h + 1) * HEAD] for h in range(NH)], axis=0).astype(BF)
    lim = jnp.zeros((8, ROWS), jnp.int32)
    for t in range(4):
        lim = jnp.where(sub == t, ends[t], lim)
    seen = jnp.concatenate([lane <= lim] * NH, axis=0)
    s0 = jnp.where(seen, nt(qs, kvo[:, 0:HEAD]), NEG)
    s1 = nt(qs, kvr[:, 0:HEAD]) + bias[ROOT]
    s2 = nt(qs, kvp[:, 0:HEAD]) + bias[PAR]
    m = jnp.maximum(
        jnp.max(s0, axis=1, keepdims=True),
        jnp.maximum(jnp.max(s1, axis=1, keepdims=True), jnp.max(s2, axis=1, keepdims=True)),
    )
    total = jnp.zeros((8 * NH, 1), F32)
    out = jnp.zeros((8 * NH, HEAD), F32)
    for s, kv in ((s0, kvo), (s1, kvr), (s2, kvp)):
        p = jnp.exp2((s - m) * C2).astype(BF)
        total = total + jnp.sum(p.astype(F32), axis=1, keepdims=True)
        out = out + nn(p, kv[:, HEAD:])
    out = (out / total).astype(BF).astype(F32)
    part = jnp.zeros((8, 1), F32)
    for h in range(NH):
        part = part + jnp.sum(out[8 * h:8 * h + 8] * w_ref[h:h + 1, :], axis=1, keepdims=True)
    mine = lax.broadcasted_iota(jnp.int32, (8, HEAD), 1) == me
    tile = jnp.where(mine, part, 0.0)
    rsend[...] = tile
    hrx[hd] = tile
    base = ids(7)
    heads = []
    for d in range(1, NH):
        c = head_copy(rsend, hrx.at[hd], base + d - 1, (hd + d) % NH)
        c.start()
        heads.append(c)
    sent += heads

    loop(4, 8, far_fwd(ROOT, kvr))
    for c in heads:
        c.wait_recv()
    total = hrx[0]
    for i in range(1, NH):
        total = total + hrx[i]
    rrow[x] = total
    base = ids(3)
    across = []
    for d in range(1, COLS):
        c = seg_copy(rrow.at[x], rrow.at[x], base + d - 1, xdev[d])
        c.start()
        across.append(c)
    sent += across
    loop(0, 3, far_fwd(PAR, kvp))
    for c in across:
        c.wait_recv()
    base = ids(7)
    along = []
    for d in range(1, ZS):
        c = seg_copy(rrow, rall.at[z], base + d - 1, zdev[d])
        c.start()
        along.append(c)
    sent += along
    for t in range(COLS):
        rall[z, t] = rrow[t]
    loop(3, 8, far_fwd(PAR, kvp))

    def fin1(h):
        inv = 1.0 / lrun[h]
        a = (oacc[h] * inv).astype(BF)
        att_ref[:, hs(h)] = a.T
        oacc[h] = a.astype(F32)
        lrun[h] = inv

    loop(0, 8, fin1)
    for c in along:
        c.wait_recv()
    rew = jnp.zeros((8, HEAD), F32)
    for i in range(ZS):
        for t in range(COLS):
            rew = rew + rall[i, t]
    scores, dr = standardize(rew, tgt_ref[...], par_ref)
    own_score = jnp.sum(jnp.where(mine, scores, 0.0), axis=1, keepdims=True)
    sc_ref[...] = own_score + jnp.zeros((8, HEAD), F32)
    own_grad = jnp.sum(jnp.where(mine, dr, 0.0), axis=1, keepdims=True)
    at = lax.broadcasted_iota(jnp.int32, (ROWS, HEAD), 0)
    sg = jnp.zeros((ROWS, HEAD), F32)
    for t in range(4):
        sg = jnp.where(at == ends[t], own_grad[t:t + 1, :], sg)
    stepg[...] = sg

    def fin2(h):
        g = (g_ref[:, hs(h)].astype(F32) + stepg[...] * w_ref[pl.ds(h, 1), :]).astype(BF)
        gt = g.T
        got[h] = gt
        dl[h] = jnp.sum(gt.astype(F32) * oacc[h], axis=0, keepdims=True)
        for b in range(3):
            fs[b, h] = jnp.exp2((mblk[b, h] - mrun[h]) * C2) * lrun[h]

    loop(0, 8, fin2)
    dka[...] = jnp.zeros((3, ROWS, HEAD), F32)
    dva[...] = jnp.zeros((3, ROWS, HEAD), F32)

    def far_bwd(b, kv, start):
        def run(h):
            f = fs[b, h]
            gp = (got[h].astype(F32) * f).astype(BF)
            p = pbuf[b, h]
            dp = nn(kv[:, HEAD:], gp)
            ds = (p.astype(F32) * (dp - dl[h] * f)).astype(BF)
            dka[b] += nn(ds, q_ref[:, hs(h)])
            dva[b] += nn(p, gp.T)
            dq = nn(kt[b], ds)
            dqt[h] = dq if start else dqt[h] + dq
        return run

    def own_bwd(h):
        f = fs[OWN, h]
        gp = (got[h].astype(F32) * f).astype(BF)
        gr = gp.T
        df = dl[h] * f
        q = q_ref[:, hs(h)]
        p1 = pbuf[OWN, h, 0:HALF, :]
        p3 = pbuf[OWN, h, HALF:, HALF:]
        d1 = (p1.astype(F32) * (nn(kvo[0:HALF, HEAD:], gp) - df)).astype(BF)
        d3 = (p3.astype(F32) * (nn(kvo[HALF:, HEAD:], gp[:, HALF:]) - df[:, HALF:])).astype(BF)
        dka[OWN, 0:HALF] += nn(d1, q)
        dka[OWN, HALF:] += nn(d3, q[HALF:])
        dva[OWN, 0:HALF] += nn(p1, gr)
        dva[OWN, HALF:] += nn(p3, gr[HALF:])
        dq = dqt[h] + nn(kt[OWN, :, 0:HALF], d1)
        dq_ref[0:HALF, hs(h)] = (dq[:, 0:HALF] * SCALE).astype(BF).T
        dqb = dq[:, HALF:] + nn(kt[OWN, :, HALF:], d3)
        dq_ref[HALF:, hs(h)] = (dqb * SCALE).astype(BF).T

    def scatter(send, take, b):
        send[:, 0:HEAD] = (dka[b] * SCALE).astype(BF)
        send[:, HEAD:] = dva[b].astype(BF)
        base = ids(3)
        out = []
        for d in range(1, COLS):
            c = seg_copy(send.at[quarter(xs[d]), :], take.at[x], base + d - 1, xdev[d])
            c.start()
            out.append(c)
        take[x] = send[quarter(x), :]
        return out

    loop(0, 8, far_bwd(ROOT, kvr, True))
    roots = scatter(grs, grx, ROOT)
    loop(0, 4, far_bwd(PAR, kvp, False))
    for c in roots:
        c.wait_recv()
    sent += roots
    rsum = grx[0].astype(F32)
    for t in range(1, COLS):
        rsum = rsum + grx[t].astype(F32)
    rrs[...] = rsum.astype(BF)
    base = ids(ZS - 1)

    def root_sum(d):
        return seg_copy(rrs, rrx.at[z], base + d - 1, x)

    for d in range(1, ZS):
        @pl.when(z == d)
        def _():
            root_sum(d).start()

    loop(4, 8, far_bwd(PAR, kvp, False))
    pars = scatter(gps, gpx, PAR)
    loop(0, 2, own_bwd)
    for c in pars:
        c.wait_recv()
    sent += pars

    row_par = [par_ref[z * COLS + t] for t in range(COLS)]
    carry = jnp.zeros((QUART, 2 * HEAD), F32)
    for t in range(COLS):
        far = (row_par[t] > 0) & (row_par[t] < z * COLS)
        carry = carry + gpx[t].astype(F32) * hot(far)
    cbuf[z] = carry.astype(BF)
    ring(cbuf, [lambda i=i: loop(2 + i, 3 + i, own_bwd) for i in range(4)])

    rsumq[...] = jnp.zeros((QUART, 2 * HEAD), BF)

    @pl.when(z == 0)
    def _():
        acc = rrs[...].astype(F32)
        for d in range(1, ZS):
            seg_copy(rrs, rrx.at[d], base + d - 1, x).wait_recv()
            acc = acc + rrx[d].astype(F32)
        rsumq[...] = acc.astype(BF)

    def incoming(c):
        seg = z * COLS + c
        acc = rsumq[...].astype(F32) * hot(seg == 0)
        for t in range(COLS):
            acc = acc + gpx[t].astype(F32) * hot((row_par[t] > 0) & (row_par[t] == seg))
        for i in range(1, ZS):
            par = par_ref[i * COLS]
            acc = acc + cbuf[i].astype(F32) * hot((par > 0) & (par == seg) & (i > z))
        return acc.astype(BF)

    base3 = ids(3)
    final = []
    for d in range(1, COLS):
        fsend[d - 1] = incoming(xs[d])
        c = seg_copy(fsend.at[d - 1], frx.at[quarter(x), :], base3 + d - 1, xdev[d])
        c.start()
        final.append(c)
    sent += final
    frx[quarter(x), :] = incoming(x)
    loop(6, 8, own_bwd)
    for c in final:
        c.wait_recv()
    dk_ref[...] = (dka[OWN] * SCALE + frx[:, 0:HEAD].astype(F32)).astype(BF)
    dv_ref[...] = (dva[OWN] + frx[:, HEAD:].astype(F32)).astype(BF)

    for c in sent:
        c.wait_send()
    for hop in range(ZS // 2):
        @pl.when(z == hop)
        def _():
            root_copy(0).wait_send()
        if hop < ZS // 2 - 1:
            @pl.when(z == (ZS - hop) % ZS)
            def _():
                root_copy(1).wait_send()
    for d in range(1, ZS):
        @pl.when(z == d)
        def _():
            root_sum(d).wait_send()


def local(queries, keys, values, out_grad, reward_weight, parent, step_ends, target):
    tgt = jnp.pad(target.T, ((0, 4), (0, HEAD - target.shape[0])))
    vmem = pl.BlockSpec(memory_space=pltpu.VMEM)
    smem = pl.BlockSpec(memory_space=pltpu.SMEM)
    wide = jax.ShapeDtypeStruct((ROWS, NH * HEAD), BF)
    slim = jax.ShapeDtypeStruct((ROWS, HEAD), BF)
    V = pltpu.VMEM
    blk = (QUART, 2 * HEAD)
    scratch = [
        V((ROWS, 2 * HEAD), BF), V((ROWS, 2 * HEAD), BF), V((ROWS, 2 * HEAD), BF),
        V((3, HEAD + 16, ROWS), BF), V((3, HEAD, ROWS), BF),
        V((3, NH, ROWS, ROWS), BF),
        V((NH, HEAD, ROWS), F32), V((NH, 1, ROWS), F32), V((NH, 1, ROWS), F32), V((3, NH, 1, ROWS), F32),
        V((NH, HEAD, ROWS), BF), V((NH, 1, ROWS), F32), V((3, NH, 1, ROWS), F32),
        V((NH, HEAD, ROWS), F32), V((3, ROWS, HEAD), F32), V((3, ROWS, HEAD), F32),
        V((COLS,) + blk, BF), V((ZS + COLS,) + blk, BF), V(blk, BF), V((COLS - 1,) + blk, BF),
        V((NH, 8, HEAD), F32), V((COLS, 8, HEAD), F32), V((ZS, COLS, 8, HEAD), F32), V((8, HEAD), F32),
        V((ROWS, HEAD), F32),
        V((ROWS, 2 * HEAD), BF), V((ROWS, 2 * HEAD), BF), V((COLS,) + blk, BF), V((COLS,) + blk, BF),
        V((ZS,) + blk, BF), V(blk, BF), V((ZS,) + blk, BF), V(blk, BF), V((COLS - 1,) + blk, BF), V((ROWS, 2 * HEAD), BF),
        pltpu.SemaphoreType.DMA((64,)), pltpu.SemaphoreType.DMA((64,)),
    ]
    att, sc, dq, dk, dv = pl.pallas_call(
        kernel,
        out_shape=(wide, jax.ShapeDtypeStruct((8, HEAD), F32), wide, slim, slim),
        in_specs=[vmem, vmem, vmem, vmem, vmem, smem, smem, vmem],
        out_specs=(vmem,) * 5,
        scratch_shapes=scratch,
        compiler_params=pltpu.CompilerParams(
            collective_id=0, has_side_effects=True, vmem_limit_bytes=56 * 1024 * 1024
        ),
        name="tree_attention",
    )(queries, keys, values, out_grad, reward_weight.reshape(NH, HEAD), parent, step_ends, tgt)
    return att, sc[0:4, 0].reshape(1, 4), dq, dk, dv


def solution(mesh):
    both = P("seg", "head")
    return jax.shard_map(
        local,
        mesh=mesh,
        in_specs=(both, both, both, both, P("head"), P(), P("seg", None), P()),
        out_specs=(both, P("seg", None), both, both, both),
        check_vma=False,
    )
```

```python
import functools
import math

import jax
import jax.numpy as jnp
from jax import lax
from jax.experimental import pallas as pl
from jax.experimental.pallas import tpu as pltpu
from jax.sharding import PartitionSpec as P

HEAD = 128
ROWS = 512
NH = 8
COLS = 4
ZS = 8
QUART = ROWS // COLS
HALF = ROWS // 2
SCALE = 1.0 / math.sqrt(HEAD)
C2 = SCALE * math.log2(math.e)
BF = jnp.bfloat16
F32 = jnp.float32
NEG = float("-inf")
MESH = pl.DeviceIdType.MESH
OWN, ROOT, PAR = 0, 1, 2


def nn(a, b):
    return jnp.dot(a, b, preferred_element_type=F32)


def nt(a, b):
    return lax.dot_general(a, b, (((1,), (1,)), ((), ())), preferred_element_type=F32)


def hot(cond):
    return jnp.where(cond, 1.0, 0.0).astype(F32)


def tn(a, b):
    return lax.dot_general(a, b, (((0,), (0,)), ((), ())), preferred_element_type=F32)


def exact(a, b):
    return jnp.dot(a, b, preferred_element_type=F32, precision=lax.Precision.HIGHEST)


def standardize(rew, tgt, par_ref):
    segs = COLS * ZS
    lane = lax.broadcasted_iota(jnp.int32, (HEAD, HEAD), 1)
    sub = lax.broadcasted_iota(jnp.int32, (HEAD, HEAD), 0)
    prow = jnp.full((HEAD, HEAD), -2.0, F32)
    for s in range(segs):
        prow = jnp.where(lane == s, par_ref[s].astype(F32), prow)
    pcol = prow.T
    inside = (lane < segs) & (sub < segs)
    sib = jnp.where(inside & (prow == pcol), 1.0, 0.0)
    up = jnp.where(inside & (prow == sub.astype(F32)), 1.0, 0.0)
    down = up.T
    cnt = jnp.maximum(jnp.sum(sib, axis=0, keepdims=True), 1.0)
    row = lax.broadcasted_iota(jnp.int32, (8, HEAD), 0)
    used = row < 4
    before = exact(rew, up)
    shifted = jnp.concatenate([before[3:4], rew[0:7]], axis=0)
    margin = jnp.where(used, rew - shifted, 0.0)
    mean = exact(margin, sib) / cnt
    cen = margin - mean
    var = exact(cen * cen, sib) / cnt
    floor = jnp.maximum(var, 0.25)
    inv = lax.rsqrt(floor)
    scores = cen * inv
    slope = jnp.where(var > 0.25, 1.0, jnp.where(var == 0.25, 0.5, 0.0))
    dvar = tgt * cen * (-0.5) * inv / floor * slope
    dcen = tgt * inv + 2.0 * cen * exact(dvar / cnt, sib)
    dmar = jnp.where(used, dcen - exact(dcen / cnt, sib), 0.0)
    back = exact(dmar, down)
    later = jnp.concatenate([dmar[1:8], dmar[0:1]], axis=0)
    later = jnp.where(row < 3, later, jnp.where(row == 3, back[0:1], 0.0))
    return scores, dmar - later


def kernel(
    reach, q_hbm, k_hbm, v_hbm, g_hbm, w_ref, par_ref, ends_ref, tgt_ref,
    att_hbm, sc_ref, dq_hbm, dk_hbm, dv_hbm,
    q_ref, g_ref, att_ref, dq_ref, dk_ref, dv_ref,
    kvo, kvr, kvp, vt, kt, pbuf, oacc, mrun, lrun, mblk, got, dl, fs, dqt, dka, dva,
    rowbuf, epart, zbuf, rootq, psend, hrx, rrow, rpart, rall, rsend, keep, tgtp,
    pst, qst, gst, ost, wrep, pick, dqst,
    grs, gps, grx, gpx, cpart, cbuf, rrs, rrx, rsumq, fsend, frx,
    ssem, rsem, lsem,
):
    me = lax.axis_index("seg")
    hd = lax.axis_index("head")
    z = me // COLS
    x = me % COLS
    xs = [(x + d) % COLS for d in range(COLS)]
    xdev = [z * COLS + c for c in xs]
    zdev = [((z + d) % ZS) * COLS + x for d in range(ZS)]
    count = [0]
    sent = []

    def ids(n):
        count[0] += n
        return count[0] - n

    def seg_copy(src, dst, i, seg, j=None):
        return pltpu.make_async_remote_copy(
            src_ref=src, dst_ref=dst, send_sem=ssem.at[i], recv_sem=rsem.at[i if j is None else j],
            device_id=(seg, hd), device_id_type=MESH,
        )

    def head_copy(src, dst, i, head):
        return pltpu.make_async_remote_copy(
            src_ref=src, dst_ref=dst, send_sem=ssem.at[i], recv_sem=rsem.at[i],
            device_id=(me, head), device_id_type=MESH,
        )

    def across(src, dst):
        base = ids(COLS - 1)
        out = []
        for d in (2, 1, 3):
            c = seg_copy(src(d), dst, base + d - 1, xdev[d])
            c.start()
            out.append(c)
        sent.extend(out)
        return out

    def arrive(copies):
        for c in copies:
            c.wait_recv()

    def hs(h):
        return pl.ds(pl.multiple_of(h * HEAD, HEAD), HEAD)

    def quarter(c):
        return pl.ds(pl.multiple_of(c * QUART, QUART), QUART)

    def loop(lo, hi, fn):
        def step(h, carry):
            fn(h)
            return carry
        n = hi - lo
        lax.fori_loop(lo, hi, step, 0, unroll=4 if n % 4 == 0 else 2 if n % 2 == 0 else 1)

    loads = [
        pltpu.make_async_copy(k_hbm, kvo.at[:, pl.ds(0, HEAD)], lsem.at[0]),
        pltpu.make_async_copy(v_hbm, kvo.at[:, pl.ds(HEAD, HEAD)], lsem.at[1]),
        pltpu.make_async_copy(q_hbm, q_ref, lsem.at[2]),
        pltpu.make_async_copy(g_hbm, g_ref, lsem.at[3]),
    ]
    for c in loads:
        c.start()
    barrier = pltpu.get_barrier_semaphore()
    for d in range(1, COLS):
        pl.semaphore_signal(barrier, inc=1, device_id=(xdev[d], hd), device_id_type=MESH)
    for d in range(1, ZS):
        pl.semaphore_signal(barrier, inc=1, device_id=(zdev[d], hd), device_id_type=MESH)
    for d in range(1, NH):
        pl.semaphore_signal(barrier, inc=1, device_id=(me, (hd + d) % NH), device_id_type=MESH)
    lane = lax.broadcasted_iota(jnp.int32, (16, ROWS), 1)
    sub = lax.broadcasted_iota(jnp.int32, (16, ROWS), 0)
    ends = [ends_ref[0, t] for t in range(4)]
    hits = jnp.zeros((16, ROWS), F32)
    lim = jnp.zeros((8, ROWS), jnp.int32)
    kept = jnp.ones((1, ROWS), F32)
    for t in range(4):
        hits = jnp.where((sub == t) & (lane == ends[t]), 1.0, hits)
        lim = jnp.where(sub[0:8] == t, ends[t], lim)
        kept = jnp.where(lane[0:1] == ends[t], 0.0, kept)
    pick[...] = hits.astype(BF)
    keep[...] = kept
    for h in range(NH):
        wrep[8 * h:8 * h + 8, :] = w_ref[h:h + 1, :] + jnp.zeros((8, HEAD), F32)
    tgtp[...] = jnp.zeros((8, HEAD), F32)
    tgtp[0:4, 0:COLS * ZS] = tgt_ref[...]
    loads[0].wait()
    loads[1].wait()
    pl.semaphore_wait(barrier, COLS - 1 + ZS - 1 + NH - 1)

    first = across(lambda d: kvo.at[quarter(xs[d]), :], rowbuf.at[x])
    rowbuf[x] = kvo[quarter(x), :]

    lowest = lax.broadcasted_iota(jnp.int32, (HALF, HALF), 0)
    diag = lowest <= lax.broadcasted_iota(jnp.int32, (HALF, HALF), 1)

    def flip(b, kv):
        kt[b] = kv[:, 0:HEAD].T
        vt[b, 0:HEAD, :] = kv[:, HEAD:].T
        vt[b, HEAD:, :] = jnp.ones((16, ROWS), BF)

    def own_fwd(h):
        q = q_ref[:, hs(h)]
        qa, qb = q[0:HALF], q[HALF:]
        ka, kb = kvo[0:HALF, 0:HEAD], kvo[HALF:, 0:HEAD]
        s1 = jnp.where(diag, nt(ka, qa), NEG)
        s2 = nt(ka, qb)
        s3 = jnp.where(diag, nt(kb, qb), NEG)
        m1 = jnp.max(s1, axis=0, keepdims=True)
        m2 = jnp.maximum(jnp.max(s2, axis=0, keepdims=True), jnp.max(s3, axis=0, keepdims=True))
        p1 = jnp.exp2((s1 - m1) * C2).astype(BF)
        p2 = jnp.exp2((s2 - m2) * C2).astype(BF)
        p3 = jnp.exp2((s3 - m2) * C2).astype(BF)
        pbuf[OWN, h, 0:HALF, 0:HALF] = p1
        pbuf[OWN, h, 0:HALF, HALF:] = p2
        pbuf[OWN, h, HALF:, HALF:] = p3
        o1 = nn(vt[OWN, :, 0:HALF], p1)
        o2 = nn(vt[OWN, :, 0:HALF], p2) + nn(vt[OWN, :, HALF:], p3)
        oacc[h, :, 0:HALF] = o1[0:HEAD]
        oacc[h, :, HALF:] = o2[0:HEAD]
        lrun[h, :, 0:HALF] = o1[HEAD:HEAD + 1]
        lrun[h, :, HALF:] = o2[HEAD:HEAD + 1]
        mrun[h, :, 0:HALF] = m1
        mrun[h, :, HALF:] = m2
        mblk[OWN, h, :, 0:HALF] = m1
        mblk[OWN, h, :, HALF:] = m2

    my_par = par_ref[me]
    bias = {
        ROOT: jnp.where(my_par >= 0, 0.0, NEG).astype(F32),
        PAR: jnp.where(my_par > 0, 0.0, NEG).astype(F32),
    }

    def far_fwd(b, kv):
        def run(h):
            s = nt(kv[:, 0:HEAD], q_ref[:, hs(h)])
            m = jnp.max(s, axis=0, keepdims=True)
            p = jnp.exp2((s - m) * C2).astype(BF)
            pbuf[b, h] = p
            o = nn(vt[b], p)
            top = m + bias[b]
            old = mrun[h]
            new = jnp.maximum(old, top)
            a = jnp.exp2((old - new) * C2)
            e = jnp.exp2((top - new) * C2)
            oacc[h] = oacc[h] * a + o[0:HEAD] * e
            lrun[h] = lrun[h] * a + o[HEAD:HEAD + 1] * e
            mrun[h] = new
            mblk[b, h] = top
        return run

    flip(OWN, kvo)
    loads[2].wait()
    loop(0, 4, own_fwd)
    arrive(first)

    rid = ids(ZS - 1)

    def root_out(d):
        return seg_copy(rootq, rootq, rid + d - 1, zdev[d], rid)

    @pl.when(z == 0)
    def _():
        rootq[...] = rowbuf[0]
        for d in (4, 3, 5, 2, 6, 1, 7):
            root_out(d).start()

    last = jnp.int32(0)
    for t in range(COLS):
        last = jnp.where(par_ref[z * COLS + t] == 0, t, last)
    epart[...] = rowbuf[last]
    base = ids(reach)
    carried = []
    for d in sorted(range(1, reach + 1), key=lambda d: -min(d, ZS - d)):
        c = seg_copy(epart, zbuf.at[d - 1], base + d - 1, zdev[d])
        c.start()
        carried.append(c)
    sent += carried
    for t in range(COLS):
        zbuf[reach + t] = rowbuf[t]
    loop(4, 8, own_fwd)
    arrive(carried)

    def place(c):
        p = jnp.maximum(par_ref[z * COLS + c], 0)
        back = jnp.clip(z - p // COLS - 1, 0, reach - 1)
        return jnp.where(p // COLS == z, reach + p % COLS, back)

    for d in range(1, COLS):
        psend[d - 1] = zbuf[place(xs[d])]
    third = across(lambda d: psend.at[d - 1], kvp.at[quarter(x), :])
    kvp[quarter(x), :] = zbuf[place(x)]

    @pl.when(z != 0)
    def _():
        root_out(1).wait_recv()

    fourth = across(lambda d: rootq, kvr.at[quarter(x), :])
    kvr[quarter(x), :] = rootq[...]
    arrive(third)
    flip(PAR, kvp)
    loop(0, 8, far_fwd(PAR, kvp))
    arrive(fourth)
    flip(ROOT, kvr)

    def spread(r):
        return jnp.concatenate([r[:, h * HEAD:(h + 1) * HEAD] for h in range(NH)], axis=0)

    qs = spread(nn(pick[...], q_ref[...])[0:8]).astype(BF)
    qst[...] = qs
    loads[3].wait()
    gst[...] = spread(nn(pick[...], g_ref[...])[0:8])
    seen = jnp.concatenate([lane[0:8] <= lim] * NH, axis=0)
    s0 = jnp.where(seen, nt(qs, kvo[:, 0:HEAD]), NEG)
    s1 = nt(qs, kvr[:, 0:HEAD]) + bias[ROOT]
    s2 = nt(qs, kvp[:, 0:HEAD]) + bias[PAR]
    m = jnp.maximum(
        jnp.max(s0, axis=1, keepdims=True),
        jnp.maximum(jnp.max(s1, axis=1, keepdims=True), jnp.max(s2, axis=1, keepdims=True)),
    )
    total = jnp.zeros((8 * NH, 1), F32)
    probs = []
    for s in (s0, s1, s2):
        p = jnp.exp2((s - m) * C2)
        total = total + jnp.sum(p, axis=1, keepdims=True)
        probs.append(p)
    inv = 1.0 / total
    out = jnp.zeros((8 * NH, HEAD), F32)
    for b, kv in ((OWN, kvo), (ROOT, kvr), (PAR, kvp)):
        p = probs[b] * inv
        pst[b] = p
        out = out + nn(p.astype(BF), kv[:, HEAD:])
    out = out.astype(BF).astype(F32)
    ost[...] = out
    terms = jnp.sum(out * wrep[...], axis=1, keepdims=True)
    part = jnp.zeros((8, 1), F32)
    for h in range(NH):
        part = part + terms[8 * h:8 * h + 8]
    mine = lax.broadcasted_iota(jnp.int32, (8, HEAD), 1) == me
    tile = jnp.where(mine, part, 0.0)
    rsend[...] = tile
    hrx[hd] = tile
    base = ids(NH - 1)
    heads = []
    for d in range(1, NH):
        c = head_copy(rsend, hrx.at[hd], base + d - 1, (hd + d) % NH)
        c.start()
        heads.append(c)
    sent += heads

    loop(0, 4, far_fwd(ROOT, kvr))
    loop(4, 6, far_fwd(ROOT, kvr))
    arrive(heads)
    total = hrx[0]
    for i in range(1, NH):
        total = total + hrx[i]
    rrow[x] = total
    rows = across(lambda d: rrow.at[x], rrow.at[x])
    loop(6, 8, far_fwd(ROOT, kvr))

    def finish(h):
        inv = 1.0 / lrun[h]
        a = (oacc[h] * inv).astype(BF)
        att_ref[:, hs(h)] = a.T
        gt = g_ref[:, hs(h)].T
        got[h] = gt
        dl[h] = jnp.sum(gt.astype(F32) * a.astype(F32), axis=0, keepdims=True)
        inv = inv * keep[...]
        for b in range(3):
            fs[b, h] = jnp.exp2((mblk[b, h] - mrun[h]) * C2) * inv

    def far_bwd(b, kv, start):
        def run(h):
            if start:
                finish(h)
            f = fs[b, h]
            gp = (got[h].astype(F32) * f).astype(BF)
            p = pbuf[b, h]
            dp = nn(kv[:, HEAD:], gp)
            ds = (p.astype(F32) * (dp - dl[h] * f)).astype(BF)
            dka[b] += nn(ds, q_ref[:, hs(h)])
            dva[b] += nn(p, gp.T)
            dq = nn(kt[b], ds)
            dqt[h] = dq if start else dqt[h] + dq
        return run

    def own_bwd(h):
        f = fs[OWN, h]
        gp = (got[h].astype(F32) * f).astype(BF)
        gr = gp.T
        df = dl[h] * f
        q = q_ref[:, hs(h)]
        p1 = pbuf[OWN, h, 0:HALF, :]
        p3 = pbuf[OWN, h, HALF:, HALF:]
        d1 = (p1.astype(F32) * (nn(kvo[0:HALF, HEAD:], gp) - df)).astype(BF)
        d3 = (p3.astype(F32) * (nn(kvo[HALF:, HEAD:], gp[:, HALF:]) - df[:, HALF:])).astype(BF)
        dka[OWN, 0:HALF] += nn(d1, q)
        dka[OWN, HALF:] += nn(d3, q[HALF:])
        dva[OWN, 0:HALF] += nn(p1, gr)
        dva[OWN, HALF:] += nn(p3, gr[HALF:])
        dq = dqt[h] + nn(kt[OWN, :, 0:HALF], d1) + tn(dqst[h], pick[...])
        dq_ref[0:HALF, hs(h)] = (dq[:, 0:HALF] * SCALE).astype(BF).T
        dqb = dq[:, HALF:] + nn(kt[OWN, :, HALF:], d3)
        dq_ref[HALF:, hs(h)] = (dqb * SCALE).astype(BF).T

    dka[...] = jnp.zeros((3, ROWS, HEAD), F32)
    dva[...] = jnp.zeros((3, ROWS, HEAD), F32)
    loop(0, 4, far_bwd(ROOT, kvr, True))
    arrive(rows)
    total = rrow[0]
    for t in range(1, COLS):
        total = total + rrow[t]
    rpart[...] = total
    base = ids(ZS - 1)
    along = []
    for d in (4, 3, 5, 2, 6, 1, 7):
        c = seg_copy(rpart, rall.at[z], base + d - 1, zdev[d])
        c.start()
        along.append(c)
    sent += along
    rall[z] = total
    loop(4, 8, far_bwd(ROOT, kvr, True))
    stores = [pltpu.make_async_copy(att_ref, att_hbm, lsem.at[0])]
    stores[0].start()
    loop(0, 2, far_bwd(PAR, kvp, False))
    arrive(along)
    rew = rall[0]
    for i in range(1, ZS):
        rew = rew + rall[i]
    scores, dr = standardize(rew, tgtp[...], par_ref)
    own_score = jnp.sum(jnp.where(mine, scores, 0.0), axis=1, keepdims=True)
    own_grad = jnp.sum(jnp.where(mine, dr, 0.0), axis=1, keepdims=True)
    at = lax.broadcasted_iota(jnp.int32, (8, HEAD), 1)
    shown = jnp.zeros((8, HEAD), F32)
    for t in range(4):
        shown = jnp.where(at == t, own_score[t:t + 1, :], shown)
    sc_ref[...] = shown

    step = jnp.where(lax.broadcasted_iota(jnp.int32, (8, 1), 0) < 4, own_grad, 0.0)
    step = jnp.concatenate([step] * NH, axis=0)
    gs = (gst[...] + step * wrep[...]).astype(BF)
    delta = jnp.sum(gs.astype(F32) * ost[...], axis=1, keepdims=True)
    dqs = jnp.zeros((8 * NH, HEAD), F32)
    for b, kv in ((ROOT, kvr), (PAR, kvp), (OWN, kvo)):
        p = pst[b]
        ds = (p * (nt(gs, kv[:, HEAD:]) - delta)).astype(BF)
        dka[b] += tn(ds, qst[...])
        dva[b] += tn(p.astype(BF), gs)
        dqs = dqs + nn(ds, kv[:, 0:HEAD])
    for h in range(NH):
        dqst[h] = jnp.concatenate([dqs[8 * h:8 * h + 8], jnp.zeros((8, HEAD), F32)], axis=0).astype(BF)

    def scatter(send, take, b):
        send[:, 0:HEAD] = (dka[b] * SCALE).astype(BF)
        send[:, HEAD:] = dva[b].astype(BF)
        out = across(lambda d: send.at[quarter(xs[d]), :], take.at[x])
        take[x] = send[quarter(x), :]
        return out

    roots = scatter(grs, grx, ROOT)
    loop(2, 8, far_bwd(PAR, kvp, False))
    pars = scatter(gps, gpx, PAR)
    arrive(roots)
    rsum = grx[0].astype(F32)
    for t in range(1, COLS):
        rsum = rsum + grx[t].astype(F32)
    rrs[...] = rsum.astype(BF)
    rsumq[...] = jnp.zeros((QUART, 2 * HEAD), BF)
    sbase = ids(1)
    rbase = ids(ZS - 1)

    @pl.when(z != 0)
    def _():
        seg_copy(rrs, rrx.at[z], sbase, x, rbase + z - 1).start()

    loop(0, 2, own_bwd)
    arrive(pars)
    row_par = [par_ref[z * COLS + t] for t in range(COLS)]
    carry = jnp.zeros((QUART, 2 * HEAD), F32)
    for t in range(COLS):
        far = (row_par[t] > 0) & (row_par[t] < z * COLS)
        carry = carry + gpx[t].astype(F32) * hot(far)
    cpart[...] = carry.astype(BF)
    base = ids(reach)
    carried = []
    for d in sorted(range(1, reach + 1), key=lambda d: -min(d, ZS - d)):
        c = seg_copy(cpart, cbuf.at[d - 1], base + d - 1, zdev[ZS - d])
        c.start()
        carried.append(c)
    sent += carried
    loop(2, 8, own_bwd)
    stores.append(pltpu.make_async_copy(dq_ref, dq_hbm, lsem.at[1]))
    stores[1].start()

    arrive(carried)

    @pl.when(z == 0)
    def _():
        acc = rrs[...].astype(F32)
        for d in range(1, ZS):
            seg_copy(rrs, rrx.at[d], sbase, x, rbase + d - 1).wait_recv()
            acc = acc + rrx[d].astype(F32)
        rsumq[...] = acc.astype(BF)

    def incoming(c):
        seg = z * COLS + c
        acc = rsumq[...].astype(F32) * hot(seg == 0)
        for t in range(COLS):
            acc = acc + gpx[t].astype(F32) * hot((row_par[t] > 0) & (row_par[t] == seg))
        for d in range(1, reach + 1):
            par = par_ref[((z + d) % ZS) * COLS]
            acc = acc + cbuf[d - 1].astype(F32) * hot((par > 0) & (par == seg) & (z + d < ZS))
        return acc.astype(BF)

    for d in range(1, COLS):
        fsend[d - 1] = incoming(xs[d])
    final = across(lambda d: fsend.at[d - 1], frx.at[quarter(x), :])
    frx[quarter(x), :] = incoming(x)
    arrive(final)
    dk_ref[...] = (dka[OWN] * SCALE + frx[:, 0:HEAD].astype(F32)).astype(BF)
    dv_ref[...] = (dva[OWN] + frx[:, HEAD:].astype(F32)).astype(BF)
    stores.append(pltpu.make_async_copy(dk_ref, dk_hbm, lsem.at[2]))
    stores.append(pltpu.make_async_copy(dv_ref, dv_hbm, lsem.at[3]))
    stores[2].start()
    stores[3].start()

    for c in sent:
        c.wait_send()

    @pl.when(z == 0)
    def _():
        for d in range(1, ZS):
            root_out(d).wait_send()

    @pl.when(z != 0)
    def _():
        seg_copy(rrs, rrx.at[z], sbase, x, rbase + z - 1).wait_send()

    for c in stores:
        c.wait()


def hand_on(a_in, q_in, k_in, v_in, s_in, a_out, q_out, k_out, v_out, s_out, sem):
    copies = []
    for src, dst, parts in ((a_in, a_out, 4), (q_in, q_out, 4), (k_in, k_out, 1), (v_in, v_out, 1)):
        n = ROWS // parts
        for i in range(parts):
            rows = pl.ds(i * n, n)
            copies.append(pltpu.make_async_copy(src.at[rows, :], dst.at[rows, :], sem.at[len(copies)]))
    for c in copies:
        c.start()
    s_out[...] = s_in[0:1, 0:4]
    for c in copies:
        c.wait()


def local(queries, keys, values, out_grad, reward_weight, parent, step_ends, target):
    vmem = pl.BlockSpec(memory_space=pltpu.VMEM)
    smem = pl.BlockSpec(memory_space=pltpu.SMEM)
    hbm = pl.BlockSpec(memory_space=pl.ANY)
    wide = jax.ShapeDtypeStruct((ROWS, NH * HEAD), BF)
    slim = jax.ShapeDtypeStruct((ROWS, HEAD), BF)
    V = pltpu.VMEM
    blk = (QUART, 2 * HEAD)
    full = (ROWS, 2 * HEAD)
    stat = (NH, 1, ROWS)
    tile = (8, HEAD)
    steps = (8 * NH, HEAD)

    def call(reach, cid):
        scratch = [
            V((ROWS, NH * HEAD), BF), V((ROWS, NH * HEAD), BF), V((ROWS, NH * HEAD), BF),
            V((ROWS, NH * HEAD), BF), V((ROWS, HEAD), BF), V((ROWS, HEAD), BF),
            V(full, BF), V(full, BF), V(full, BF),
            V((3, HEAD + 16, ROWS), BF), V((3, HEAD, ROWS), BF),
            V((3, NH, ROWS, ROWS), BF),
            V((NH, HEAD, ROWS), F32), V(stat, F32), V(stat, F32), V((3,) + stat, F32),
            V((NH, HEAD, ROWS), BF), V(stat, F32), V((3,) + stat, F32),
            V((NH, HEAD, ROWS), F32), V((3, ROWS, HEAD), F32), V((3, ROWS, HEAD), F32),
            V((COLS,) + blk, BF), V(blk, BF), V((reach + COLS,) + blk, BF), V(blk, BF), V((COLS - 1,) + blk, BF),
            V((NH,) + tile, F32), V((COLS,) + tile, F32), V(tile, F32), V((ZS,) + tile, F32), V(tile, F32),
            V((1, ROWS), F32), V(tile, F32),
            V((3, 8 * NH, ROWS), F32), V(steps, BF), V(steps, F32), V(steps, F32), V(steps, F32),
            V((16, ROWS), BF), V((NH, 16, HEAD), BF),
            V(full, BF), V(full, BF), V((COLS,) + blk, BF), V((COLS,) + blk, BF),
            V(blk, BF), V((reach,) + blk, BF), V(blk, BF), V((ZS,) + blk, BF), V(blk, BF),
            V((COLS - 1,) + blk, BF), V(full, BF),
            pltpu.SemaphoreType.DMA((80,)), pltpu.SemaphoreType.DMA((80,)), pltpu.SemaphoreType.DMA((4,)),
        ]
        return pl.pallas_call(
            functools.partial(kernel, reach),
            out_shape=(wide, jax.ShapeDtypeStruct(tile, F32), wide, slim, slim),
            in_specs=[hbm, hbm, hbm, hbm, vmem, smem, smem, vmem],
            out_specs=(hbm, vmem, hbm, hbm, hbm),
            scratch_shapes=scratch,
            compiler_params=pltpu.CompilerParams(
                collective_id=cid, has_side_effects=True, vmem_limit_bytes=40 * 1024 * 1024
            ),
            name="tree_attention_%d" % reach,
        )

    seg = jnp.arange(parent.shape[0], dtype=jnp.int32)
    distant = jnp.any((parent > 0) & (seg // COLS - parent // COLS > 1))
    att, sc, dq, dk, dv = lax.cond(
        distant, call(ZS - 1, 1), call(1, 0),
        queries, keys, values, out_grad, reward_weight.reshape(NH, HEAD), parent, step_ends, target.T,
    )
    return pl.pallas_call(
        hand_on,
        out_shape=(wide, wide, slim, slim, jax.ShapeDtypeStruct((1, 4), F32)),
        in_specs=[hbm, hbm, hbm, hbm, vmem],
        out_specs=(hbm, hbm, hbm, hbm, vmem),
        scratch_shapes=[pltpu.SemaphoreType.DMA((10,))],
        name="hand_on",
    )(att, dq, dk, dv, sc)


def whole(*args):
    att, dq, dk, dv, sc = local(*args)
    return att, sc, dq, dk, dv


def solution(mesh):
    both = P("seg", "head")
    return jax.shard_map(
        whole,
        mesh=mesh,
        in_specs=(both, both, both, both, P("head"), P(), P("seg", None), P()),
        out_specs=(both, P("seg", None), both, both, both),
        check_vma=False,
    )
```

```python
import functools
import math

import jax
import jax.numpy as jnp
from jax import lax
from jax.experimental import pallas as pl
from jax.experimental.pallas import tpu as pltpu
from jax.sharding import PartitionSpec as P

HEAD = 128
ROWS = 512
NH = 8
COLS = 4
ZS = 8
QUART = ROWS // COLS
HALF = ROWS // 2
SCALE = 1.0 / math.sqrt(HEAD)
C2 = SCALE * math.log2(math.e)
BF = jnp.bfloat16
F32 = jnp.float32
NEG = float("-inf")
MESH = pl.DeviceIdType.MESH
OWN, ROOT, PAR = 0, 1, 2


def nn(a, b):
    return jnp.dot(a, b, preferred_element_type=F32)


def nt(a, b):
    return lax.dot_general(a, b, (((1,), (1,)), ((), ())), preferred_element_type=F32)


def hot(cond):
    return jnp.where(cond, 1.0, 0.0).astype(F32)


def tn(a, b):
    return lax.dot_general(a, b, (((0,), (0,)), ((), ())), preferred_element_type=F32)


def exact(a, m):
    hi = a.astype(BF).astype(F32)
    mid = (a - hi).astype(BF).astype(F32)
    low = a - hi - mid
    parts = jnp.concatenate([hi, mid, low, jnp.zeros((8, HEAD), F32)], axis=0).astype(BF)
    r = nn(parts, m)
    return (r[16:24] + r[8:16]) + r[0:8]


def tree_matrices(par_ref):
    segs = COLS * ZS
    lane = lax.broadcasted_iota(jnp.int32, (HEAD, HEAD), 1)
    sub = lax.broadcasted_iota(jnp.int32, (HEAD, HEAD), 0)
    prow = jnp.full((1, HEAD), -2.0, F32)
    for s in range(segs):
        prow = jnp.where(lane[0:1] == s, par_ref[s].astype(F32), prow)
    prow = prow + jnp.zeros((HEAD, HEAD), F32)
    inside = (lane < segs) & (sub < segs)
    sib = jnp.where(inside & (prow == prow.T), 1.0, 0.0)
    up = jnp.where(inside & (prow == sub.astype(F32)), 1.0, 0.0)
    cnt = jnp.maximum(jnp.sum(sib, axis=0, keepdims=True), 1.0)
    return sib, up, up.T, cnt


def standardize(rew, tgt, sib, up, down, cnt):
    row = lax.broadcasted_iota(jnp.int32, (8, HEAD), 0)
    used = row < 4
    before = exact(rew, up)
    shifted = jnp.concatenate([before[3:4], rew[0:7]], axis=0)
    margin = jnp.where(used, rew - shifted, 0.0)
    mean = exact(margin, sib) / cnt
    cen = margin - mean
    var = exact(cen * cen, sib) / cnt
    floor = jnp.maximum(var, 0.25)
    inv = lax.rsqrt(floor)
    scores = cen * inv
    slope = jnp.where(var > 0.25, 1.0, jnp.where(var == 0.25, 0.5, 0.0))
    dvar = tgt * cen * (-0.5) * inv / floor * slope
    dcen = tgt * inv + 2.0 * cen * exact(dvar / cnt, sib)
    dmar = jnp.where(used, dcen - exact(dcen / cnt, sib), 0.0)
    back = exact(dmar, down)
    later = jnp.concatenate([dmar[1:8], dmar[0:1]], axis=0)
    later = jnp.where(row < 3, later, jnp.where(row == 3, back[0:1], 0.0))
    return scores, dmar - later


def kernel(
    reach, q_hbm, k_hbm, v_hbm, g_hbm, w_ref, par_ref, ends_ref, tgt_ref,
    att_hbm, sc_ref, dq_hbm, dk_hbm, dv_hbm,
    q_ref, g_ref, att_ref, dq_ref, dk_ref, dv_ref,
    ko, vo, kr, vr, kp, vp, vt, kt, pbuf, oacc, mrun, lrun, mblk, got, att, dl, fs, dka, dva,
    row0, row1, ep0, ep1, zb0, zb1, rq0, rq1, ps0, ps1, hrx, rrow, rpart, rall, rsend, keep, tgtp,
    pst, qst, gst, ost, wrep, pick, dqst, sibs, ups, downs, cnts,
    grs0, grs1, gps0, gps1, grx0, grx1, gpx0, gpx1, cp0, cp1, cb0, cb1,
    rrs0, rrs1, rrx0, rrx1, rsq0, rsq1, fs0, fs1, frx0, frx1,
    intx, inrx, pc0, pc1, ssem, rsem, lsem,
):
    kvo, kvr, kvp = (ko, vo), (kr, vr), (kp, vp)
    rowbuf, epart, zbuf, rootq, psend = (row0, row1), (ep0, ep1), (zb0, zb1), (rq0, rq1), (ps0, ps1)
    grs, gps, grx, gpx = (grs0, grs1), (gps0, gps1), (grx0, grx1), (gpx0, gpx1)
    cpart, cbuf, rrs, rrx = (cp0, cp1), (cb0, cb1), (rrs0, rrs1), (rrx0, rrx1)
    rsumq, fsend, frx = (rsq0, rsq1), (fs0, fs1), (frx0, frx1)
    me = lax.axis_index("seg")
    hd = lax.axis_index("head")
    z = me // COLS
    x = me % COLS
    xs = [(x + d) % COLS for d in range(COLS)]
    xdev = [z * COLS + c for c in xs]
    zdev = [((z + d) % ZS) * COLS + x for d in range(ZS)]
    count = [0]
    sent = []

    def ids(n):
        count[0] += n
        return count[0] - n

    def seg_copy(src, dst, i, seg, j=None):
        return pltpu.make_async_remote_copy(
            src_ref=src, dst_ref=dst, send_sem=ssem.at[i], recv_sem=rsem.at[i if j is None else j],
            device_id=(seg, hd), device_id_type=MESH,
        )

    def head_copy(src, dst, i, head):
        return pltpu.make_async_remote_copy(
            src_ref=src, dst_ref=dst, send_sem=ssem.at[i], recv_sem=rsem.at[i],
            device_id=(me, head), device_id_type=MESH,
        )

    def across(src, dst):
        base = ids(COLS - 1)
        out = []
        for d in (2, 1, 3):
            c = seg_copy(src(d), dst, base + d - 1, xdev[d])
            c.start()
            out.append(c)
        sent.extend(out)
        return out

    def arrive(copies):
        for c in copies:
            c.wait_recv()

    def hs(h):
        return pl.ds(pl.multiple_of(h * HEAD, HEAD), HEAD)

    def quarter(c):
        return pl.ds(pl.multiple_of(c * QUART, QUART), QUART)

    def loop(lo, hi, fn):
        def step(h, carry):
            fn(h)
            return carry
        n = hi - lo
        lax.fori_loop(lo, hi, step, 0, unroll=1 if reach > 1 else 4 if n % 4 == 0 else 2 if n % 2 == 0 else 1)

    loads = [
        pltpu.make_async_copy(k_hbm, ko, lsem.at[0]),
        pltpu.make_async_copy(v_hbm, vo, lsem.at[1]),
        pltpu.make_async_copy(q_hbm, q_ref, lsem.at[2]),
        pltpu.make_async_copy(g_hbm, g_ref, lsem.at[3]),
    ]
    for c in loads:
        c.start()
    barrier = pltpu.get_barrier_semaphore()
    for d in range(1, COLS):
        pl.semaphore_signal(barrier, inc=1, device_id=(xdev[d], hd), device_id_type=MESH)
    for d in range(1, ZS):
        pl.semaphore_signal(barrier, inc=1, device_id=(zdev[d], hd), device_id_type=MESH)
    for d in range(1, NH):
        pl.semaphore_signal(barrier, inc=1, device_id=(me, (hd + d) % NH), device_id_type=MESH)
    lane = lax.broadcasted_iota(jnp.int32, (16, ROWS), 1)
    sub = lax.broadcasted_iota(jnp.int32, (16, ROWS), 0)
    ends = [ends_ref[0, t] for t in range(4)]
    hits = jnp.zeros((16, ROWS), F32)
    lim = jnp.zeros((8, ROWS), jnp.int32)
    kept = jnp.ones((1, ROWS), F32)
    for t in range(4):
        hits = jnp.where((sub == t) & (lane == ends[t]), 1.0, hits)
        lim = jnp.where(sub[0:8] == t, ends[t], lim)
        kept = jnp.where(lane[0:1] == ends[t], 0.0, kept)
    pick[...] = hits.astype(BF)
    keep[...] = kept
    for h in range(NH):
        wrep[8 * h:8 * h + 8, :] = w_ref[h:h + 1, :] + jnp.zeros((8, HEAD), F32)
    tgtp[...] = jnp.zeros((8, HEAD), F32)
    tgtp[0:4, 0:COLS * ZS] = tgt_ref[...]
    pl.semaphore_wait(barrier, COLS - 1 + ZS - 1 + NH - 1)

    given = (k_hbm, v_hbm)
    first = [across(lambda d: given[p].at[quarter(xs[d]), :], rowbuf[p].at[x]) for p in (0, 1)]
    for p in (0, 1):
        loads[p].wait()
        rowbuf[p][x] = kvo[p][quarter(x), :]

    lowest = lax.broadcasted_iota(jnp.int32, (HALF, HALF), 0)
    diag = lowest <= lax.broadcasted_iota(jnp.int32, (HALF, HALF), 1)

    def flip(b, kv):
        kt[b] = kv[0][...].T
        vt[b, 0:HEAD, :] = kv[1][...].T
        vt[b, HEAD:, :] = jnp.ones((16, ROWS), BF)

    def own_fwd(h):
        q = q_ref[:, hs(h)]
        qa, qb = q[0:HALF], q[HALF:]
        ka, kb = ko[0:HALF], ko[HALF:]
        s1 = jnp.where(diag, nt(ka, qa), NEG)
        s2 = nt(ka, qb)
        s3 = jnp.where(diag, nt(kb, qb), NEG)
        m1 = jnp.max(s1, axis=0, keepdims=True)
        m2 = jnp.maximum(jnp.max(s2, axis=0, keepdims=True), jnp.max(s3, axis=0, keepdims=True))
        p1 = jnp.exp2((s1 - m1) * C2).astype(BF)
        p2 = jnp.exp2((s2 - m2) * C2).astype(BF)
        p3 = jnp.exp2((s3 - m2) * C2).astype(BF)
        pbuf[OWN, h, 0:HALF, 0:HALF] = p1
        pbuf[OWN, h, 0:HALF, HALF:] = p2
        pbuf[OWN, h, HALF:, HALF:] = p3
        o1 = nn(vt[OWN, :, 0:HALF], p1)
        o2 = nn(vt[OWN, :, 0:HALF], p2) + nn(vt[OWN, :, HALF:], p3)
        oacc[h, :, 0:HALF] = o1[0:HEAD]
        oacc[h, :, HALF:] = o2[0:HEAD]
        lrun[h, :, 0:HALF] = o1[HEAD:HEAD + 1]
        lrun[h, :, HALF:] = o2[HEAD:HEAD + 1]
        mrun[h, :, 0:HALF] = m1
        mrun[h, :, HALF:] = m2
        mblk[OWN, h, :, 0:HALF] = m1
        mblk[OWN, h, :, HALF:] = m2

    my_par = par_ref[me]
    bias = {
        ROOT: jnp.where(my_par >= 0, 0.0, NEG).astype(F32),
        PAR: jnp.where(my_par > 0, 0.0, NEG).astype(F32),
    }

    def far_fwd(b, kv):
        def run(h):
            s = nt(kv[0][...], q_ref[:, hs(h)])
            m = jnp.max(s, axis=0, keepdims=True)
            p = jnp.exp2((s - m) * C2).astype(BF)
            pbuf[b, h] = p
            o = nn(vt[b], p)
            top = m + bias[b]
            old = mrun[h]
            new = jnp.maximum(old, top)
            a = jnp.exp2((old - new) * C2)
            e = jnp.exp2((top - new) * C2)
            oacc[h] = oacc[h] * a + o[0:HEAD] * e
            lrun[h] = lrun[h] * a + o[HEAD:HEAD + 1] * e
            mrun[h] = new
            mblk[b, h] = top
        return run

    flip(OWN, kvo)
    loads[2].wait()
    loop(0, 4, own_fwd)

    rid = ids(2 * (ZS - 1))

    def root_out(d, p):
        i = rid + p * (ZS - 1)
        return seg_copy(rootq[p], rootq[p], i + d - 1, zdev[d], i)

    last = jnp.int32(0)
    for t in range(COLS):
        last = jnp.where(par_ref[z * COLS + t] == 0, t, last)
    near_first = sorted(range(1, reach + 1), key=lambda d: -min(d, ZS - d))
    carried = [[], []]
    for p in (0, 1):
        arrive(first[p])

        epart[p][...] = rowbuf[p][last]
        base = ids(reach)
        for d in near_first:
            c = seg_copy(epart[p], zbuf[p].at[d - 1], base + d - 1, zdev[d])
            c.start()
            carried[p].append(c)
        sent += carried[p]
        @pl.when(z == 0)
        def _():
            rootq[p][...] = rowbuf[p][0]
            for d in (4, 3, 5, 2, 6, 1, 7):
                root_out(d, p).start()

        for t in range(COLS):
            zbuf[p][reach + t] = rowbuf[p][t]
    loop(4, 8, own_fwd)

    def spread(r):
        return jnp.concatenate([r[:, h * HEAD:(h + 1) * HEAD] for h in range(NH)], axis=0)

    qst[...] = spread(nn(pick[...], q_ref[...])[0:8]).astype(BF)
    seen = jnp.concatenate([lane[0:8] <= lim] * NH, axis=0)
    pst[OWN] = jnp.where(seen, nt(qst[...], ko[...]), NEG)

    def place(c):
        p = jnp.maximum(par_ref[z * COLS + c], 0)
        back = jnp.clip(z - p // COLS - 1, 0, reach - 1)
        return jnp.where(p // COLS == z, reach + p % COLS, back)

    third = []
    for p in (0, 1):
        arrive(carried[p])
        for d in range(1, COLS):
            psend[p][d - 1] = zbuf[p][place(xs[d])]
        third.append(across(lambda d: psend[p].at[d - 1], kvp[p].at[quarter(x), :]))
        kvp[p][quarter(x), :] = zbuf[p][place(x)]
    loads[3].wait()

    def turn(h):
        got[h] = g_ref[:, hs(h)].T

    loop(0, 8, turn)
    gst[...] = spread(nn(pick[...], g_ref[...])[0:8]).astype(BF)
    sib, up, down, cnt = tree_matrices(par_ref)
    sibs[...] = sib.astype(BF)
    ups[...] = up.astype(BF)
    downs[...] = down.astype(BF)
    cnts[...] = cnt
    fourth = []
    for p in (0, 1):
        @pl.when(z != 0)
        def _():
            root_out(1, p).wait_recv()

        fourth.append(across(lambda d: rootq[p], kvr[p].at[quarter(x), :]))
        kvr[p][quarter(x), :] = rootq[p][...]
    arrive(third[0])
    pst[PAR] = nt(qst[...], kp[...]) + bias[PAR]
    arrive(third[1])
    flip(PAR, kvp)
    loop(0, 8, far_fwd(PAR, kvp))
    arrive(fourth[0])
    pst[ROOT] = nt(qst[...], kr[...]) + bias[ROOT]
    arrive(fourth[1])

    m = jnp.maximum(
        jnp.max(pst[OWN], axis=1, keepdims=True),
        jnp.maximum(jnp.max(pst[ROOT], axis=1, keepdims=True), jnp.max(pst[PAR], axis=1, keepdims=True)),
    )
    total = jnp.zeros((8 * NH, 1), F32)
    for b in (OWN, ROOT, PAR):
        p = jnp.exp2((pst[b] - m) * C2)
        total = total + jnp.sum(p, axis=1, keepdims=True)
        pst[b] = p
    inv = 1.0 / total
    out = jnp.zeros((8 * NH, HEAD), F32)
    for b, kv in ((OWN, kvo), (ROOT, kvr), (PAR, kvp)):
        p = pst[b] * inv
        pst[b] = p
        out = out + nn(p.astype(BF), kv[1][...])
    out = out.astype(BF).astype(F32)
    ost[...] = out

    def pack(c):
        return [
            qst[...], gst[...], out.astype(BF),
            pst[ROOT, :, quarter(c)].astype(BF), pst[PAR, :, quarter(c)].astype(BF),
        ]

    for i, v in enumerate(pack(x)):
        inrx[x, i] = v
    for d in range(1, COLS):
        for i, v in enumerate(pack(xs[d])):
            intx[d - 1, i] = v
    terms = jnp.sum(out * wrep[...], axis=1, keepdims=True)
    part = jnp.zeros((8, 1), F32)
    for h in range(NH):
        part = part + terms[8 * h:8 * h + 8]
    mine = lax.broadcasted_iota(jnp.int32, (8, HEAD), 1) == me
    tile = jnp.where(mine, part, 0.0)
    rsend[...] = tile
    hrx[hd] = tile
    base = ids(NH - 1)
    heads = []
    for d in range(1, NH):
        c = head_copy(rsend, hrx.at[hd], base + d - 1, (hd + d) % NH)
        c.start()
        heads.append(c)
    sent += heads
    infos = across(lambda d: intx.at[d - 1], inrx.at[x])

    flip(ROOT, kvr)
    loop(0, 4, far_fwd(ROOT, kvr))
    loop(4, 6, far_fwd(ROOT, kvr))
    arrive(heads)
    total = hrx[0]
    for i in range(1, NH):
        total = total + hrx[i]
    rrow[x] = total
    rows = across(lambda d: rrow.at[x], rrow.at[x])
    loop(6, 8, far_fwd(ROOT, kvr))

    def finish(h):
        inv = 1.0 / lrun[h]
        a = (oacc[h] * inv).astype(BF)
        att[h] = a
        dl[h] = jnp.sum(got[h].astype(F32) * a.astype(F32), axis=0, keepdims=True)
        inv = inv * keep[...]
        for b in range(3):
            fs[b, h] = jnp.exp2((mblk[b, h] - mrun[h]) * C2) * inv

    def far_bwd(b, kv, start):
        def run(h):
            if start:
                finish(h)
            f = fs[b, h]
            gp = (got[h].astype(F32) * f).astype(BF)
            p = pbuf[b, h]
            dp = nn(kv[1][...], gp)
            ds = (p.astype(F32) * (dp - dl[h] * f)).astype(BF)
            pbuf[b, h] = ds
            dka[b] += nn(ds, q_ref[:, hs(h)])
            dva[b] += nn(p, gp.T)
        return run

    def own_bwd(h):
        f = fs[OWN, h]
        gp = (got[h].astype(F32) * f).astype(BF)
        gr = gp.T
        df = dl[h] * f
        q = q_ref[:, hs(h)]
        p1 = pbuf[OWN, h, 0:HALF, :]
        p3 = pbuf[OWN, h, HALF:, HALF:]
        d1 = (p1.astype(F32) * (nn(vo[0:HALF], gp) - df)).astype(BF)
        d3 = (p3.astype(F32) * (nn(vo[HALF:], gp[:, HALF:]) - df[:, HALF:])).astype(BF)
        dka[OWN, 0:HALF] += nn(d1, q)
        dka[OWN, HALF:] += nn(d3, q[HALF:])
        dva[OWN, 0:HALF] += nn(p1, gr)
        dva[OWN, HALF:] += nn(p3, gr[HALF:])
        far = nn(kt[ROOT], pbuf[ROOT, h]) + nn(kt[PAR], pbuf[PAR, h])
        dq = far + nn(kt[OWN, :, 0:HALF], d1)
        dq_ref[0:HALF, hs(h)] = (dq[:, 0:HALF] * SCALE).astype(BF).T
        dqb = dq[:, HALF:] + nn(kt[OWN, :, HALF:], d3)
        dq_ref[HALF:, hs(h)] = (dqb * SCALE).astype(BF).T
        att_ref[:, hs(h)] = att[h].T

    dka[...] = jnp.zeros((3, ROWS, HEAD), F32)
    dva[...] = jnp.zeros((3, ROWS, HEAD), F32)
    loop(0, 4, far_bwd(ROOT, kvr, True))
    arrive(rows)
    total = rrow[0]
    for t in range(1, COLS):
        total = total + rrow[t]
    rpart[...] = total
    base = ids(ZS - 1)
    along = []
    for d in (4, 3, 5, 2, 6, 1, 7):
        c = seg_copy(rpart, rall.at[z], base + d - 1, zdev[d])
        c.start()
        along.append(c)
    sent += along
    rall[z] = total
    loop(4, 8, far_bwd(ROOT, kvr, True))

    def scatter(send, take, b):
        out = []
        for p in (0, 1):
            send[p][...] = (dka[b] * SCALE).astype(BF) if p == 0 else dva[b].astype(BF)
            out.append(across(lambda d: send[p].at[quarter(xs[d]), :], take[p].at[x]))
            take[p][x] = send[p][quarter(x), :]
        return out

    roots = scatter(grs, grx, ROOT)
    loop(0, 8, far_bwd(PAR, kvp, False))
    pars = scatter(gps, gpx, PAR)
    arrive(along)
    rew = rall[0]
    for i in range(1, ZS):
        rew = rew + rall[i]
    scores, dr = standardize(rew, tgtp[...], sibs[...], ups[...], downs[...], cnts[...])

    def step_grad(seg, g, o):
        here = lax.broadcasted_iota(jnp.int32, (8, HEAD), 1) == seg
        own = jnp.sum(jnp.where(here, dr, 0.0), axis=1, keepdims=True)
        own = jnp.where(lax.broadcasted_iota(jnp.int32, (8, 1), 0) < 4, own, 0.0)
        gs = (g.astype(F32) + jnp.concatenate([own] * NH, axis=0) * wrep[...]).astype(BF)
        return gs, jnp.sum(gs.astype(F32) * o.astype(F32), axis=1, keepdims=True)

    def share(p, v, gs, delta, q):
        ds = (p.astype(F32) * (nt(gs, v) - delta)).astype(BF)
        return tn(ds, q) * SCALE, tn(p, gs)

    arrive(infos)
    grads = [step_grad(z * COLS + t, inrx[t, 1], inrx[t, 2]) for t in range(COLS)]
    rootk, rootv = share(
        jnp.concatenate([inrx[t, 3] for t in range(COLS)], axis=0), rootq[1][...],
        jnp.concatenate([gs for gs, _ in grads], axis=0),
        jnp.concatenate([delta for _, delta in grads], axis=0),
        jnp.concatenate([inrx[t, 0] for t in range(COLS)], axis=0),
    )
    rootc = (rootk, rootv)
    sbase = ids(2)
    rbase = ids(2 * (ZS - 1))

    def root_sum(p, slot, i):
        return seg_copy(rrs[p], rrx[p].at[slot], sbase + p, x, rbase + p * (ZS - 1) + i - 1)

    for p in (0, 1):
        arrive(roots[p])
        rsum = grx[p][0].astype(F32)
        for t in range(1, COLS):
            rsum = rsum + grx[p][t].astype(F32)
        rsum = rsum + rootc[p]
        rrs[p][...] = rsum.astype(BF)
        rsumq[p][...] = jnp.zeros((QUART, HEAD), BF)

        @pl.when(z != 0)
        def _():
            root_sum(p, z, z).start()

    loop(0, 2, own_bwd)
    for t in range(COLS):
        gs, delta = grads[t]
        pk, pv = share(inrx[t, 4], zbuf[1][place(t)], gs, delta, inrx[t, 0])
        pc0[t] = pk
        pc1[t] = pv
    parc = (pc0, pc1)
    row_par = [par_ref[z * COLS + t] for t in range(COLS)]
    carried = [[], []]
    for p in (0, 1):
        arrive(pars[p])
        carry = jnp.zeros((QUART, HEAD), F32)
        for t in range(COLS):
            far = (row_par[t] > 0) & (row_par[t] < z * COLS)
            gpc = gpx[p][t].astype(F32) + parc[p][t]
            parc[p][t] = gpc
            carry = carry + gpc * hot(far)
        cpart[p][...] = carry.astype(BF)
        base = ids(reach)
        for d in near_first:
            c = seg_copy(cpart[p], cbuf[p].at[d - 1], base + d - 1, zdev[ZS - d])
            c.start()
            carried[p].append(c)
        sent += carried[p]
    loop(2, 8, own_bwd)

    gs, delta = step_grad(me, gst[...], ost[...])
    dqs = jnp.zeros((8 * NH, HEAD), F32)
    for b, kv in ((ROOT, kvr), (PAR, kvp), (OWN, kvo)):
        p = pst[b]
        ds = (p * (nt(gs, kv[1][...]) - delta)).astype(BF)
        dqs = dqs + nn(ds, kv[0][...])
        if b == OWN:
            dka[OWN] += tn(ds, qst[...])
            dva[OWN] += tn(p.astype(BF), gs)
    for h in range(NH):
        rows16 = jnp.concatenate([dqs[8 * h:8 * h + 8], jnp.zeros((8, HEAD), F32)], axis=0)
        dqst[h] = (rows16 * SCALE).astype(BF)

    def step_dq(h):
        add = tn(pick[...], dqst[h])
        dq_ref[:, hs(h)] = (dq_ref[:, hs(h)].astype(F32) + add).astype(BF)

    loop(0, 8, step_dq)
    own_score = jnp.sum(jnp.where(mine, scores, 0.0), axis=1, keepdims=True)
    at = lax.broadcasted_iota(jnp.int32, (8, HEAD), 1)
    shown = jnp.zeros((8, HEAD), F32)
    for t in range(4):
        shown = jnp.where(at == t, own_score[t:t + 1, :], shown)
    sc_ref[...] = shown[0:1, 0:4]
    stores = [
        pltpu.make_async_copy(att_ref, att_hbm, lsem.at[0]),
        pltpu.make_async_copy(dq_ref, dq_hbm, lsem.at[1]),
    ]
    stores[0].start()
    stores[1].start()

    def incoming(c, p):
        seg = z * COLS + c
        acc = rsumq[p][...].astype(F32) * hot(seg == 0)
        for t in range(COLS):
            acc = acc + parc[p][t] * hot((row_par[t] > 0) & (row_par[t] == seg))
        for d in range(1, reach + 1):
            par = par_ref[((z + d) % ZS) * COLS]
            acc = acc + cbuf[p][d - 1].astype(F32) * hot((par > 0) & (par == seg) & (z + d < ZS))
        return acc.astype(BF)

    final = []
    for p in (0, 1):
        arrive(carried[p])

        @pl.when(z == 0)
        def _():
            acc = rrs[p][...].astype(F32)
            for d in range(1, ZS):
                root_sum(p, d, d).wait_recv()
                acc = acc + rrx[p][d].astype(F32)
            rsumq[p][...] = acc.astype(BF)

        for d in range(1, COLS):
            fsend[p][d - 1] = incoming(xs[d], p)
        final.append(across(lambda d: fsend[p].at[d - 1], frx[p].at[quarter(x), :]))
        frx[p][quarter(x), :] = incoming(x, p)
    arrive(final[0])
    dk_ref[...] = (dka[OWN] * SCALE + frx[0][...].astype(F32)).astype(BF)
    stores.append(pltpu.make_async_copy(dk_ref, dk_hbm, lsem.at[2]))
    stores[2].start()
    arrive(final[1])
    dv_ref[...] = (dva[OWN] + frx[1][...].astype(F32)).astype(BF)
    stores.append(pltpu.make_async_copy(dv_ref, dv_hbm, lsem.at[3]))
    stores[3].start()

    for c in sent:
        c.wait_send()

    @pl.when(z == 0)
    def _():
        for p in (0, 1):
            for d in range(1, ZS):
                root_out(d, p).wait_send()

    @pl.when(z != 0)
    def _():
        for p in (0, 1):
            root_sum(p, z, z).wait_send()

    for c in stores:
        c.wait()


def hand_on(a_in, q_in, k_in, v_in, s_in, a_out, q_out, k_out, v_out, s_out, sem):
    copies = []
    for src, dst, parts in ((a_in, a_out, 4), (q_in, q_out, 4), (k_in, k_out, 1), (v_in, v_out, 1)):
        n = ROWS // parts
        for i in range(parts):
            rows = pl.ds(i * n, n)
            copies.append(pltpu.make_async_copy(src.at[rows, :], dst.at[rows, :], sem.at[len(copies)]))
    copies.append(pltpu.make_async_copy(s_in, s_out, sem.at[len(copies)]))
    for c in copies:
        c.start()
    for c in copies:
        c.wait()


def local(queries, keys, values, out_grad, reward_weight, parent, step_ends, target):
    vmem = pl.BlockSpec(memory_space=pltpu.VMEM)
    smem = pl.BlockSpec(memory_space=pltpu.SMEM)
    hbm = pl.BlockSpec(memory_space=pl.ANY)
    wide = jax.ShapeDtypeStruct((ROWS, NH * HEAD), BF)
    slim = jax.ShapeDtypeStruct((ROWS, HEAD), BF)
    V = pltpu.VMEM
    blk = (QUART, HEAD)
    full = (ROWS, HEAD)
    stat = (NH, 1, ROWS)
    tile = (8, HEAD)
    steps = (8 * NH, HEAD)

    def two(shape):
        return (V(shape, BF), V(shape, BF))

    def call(reach, cid):
        scratch = [
            V((ROWS, NH * HEAD), BF), V((ROWS, NH * HEAD), BF), V((ROWS, NH * HEAD), BF),
            V((ROWS, NH * HEAD), BF), V((ROWS, HEAD), BF), V((ROWS, HEAD), BF),
            *two(full) * 3,
            V((3, HEAD + 16, ROWS), BF), V((3, HEAD, ROWS), BF),
            V((3, NH, ROWS, ROWS), BF),
            V((NH, HEAD, ROWS), F32), V(stat, F32), V(stat, F32), V((3,) + stat, F32),
            V((NH, HEAD, ROWS), BF), V((NH, HEAD, ROWS), BF), V(stat, F32), V((3,) + stat, F32),
            V((3, ROWS, HEAD), F32), V((3, ROWS, HEAD), F32),
            *two((COLS,) + blk), *two(blk), *two((reach + COLS,) + blk), *two(blk), *two((COLS - 1,) + blk),
            V((NH,) + tile, F32), V((COLS,) + tile, F32), V(tile, F32), V((ZS,) + tile, F32), V(tile, F32),
            V((1, ROWS), F32), V(tile, F32),
            V((3, 8 * NH, ROWS), F32), V(steps, BF), V(steps, BF), V(steps, F32), V(steps, F32),
            V((16, ROWS), BF), V((NH, 16, HEAD), BF),
            V((HEAD, HEAD), BF), V((HEAD, HEAD), BF), V((HEAD, HEAD), BF), V((1, HEAD), F32),
            *two(full) * 2, *two((COLS,) + blk) * 2,
            *two(blk), *two((reach,) + blk), *two(blk), *two((ZS,) + blk), *two(blk),
            *two((COLS - 1,) + blk), *two(full),
            V((COLS - 1, 5) + steps, BF), V((COLS, 5) + steps, BF),
            V((COLS,) + blk, F32), V((COLS,) + blk, F32),
            pltpu.SemaphoreType.DMA((128,)), pltpu.SemaphoreType.DMA((128,)), pltpu.SemaphoreType.DMA((4,)),
        ]
        return pl.pallas_call(
            functools.partial(kernel, reach),
            out_shape=(wide, jax.ShapeDtypeStruct((1, 4), F32), wide, slim, slim),
            in_specs=[hbm, hbm, hbm, hbm, vmem, smem, smem, vmem],
            out_specs=(hbm, vmem, hbm, hbm, hbm),
            scratch_shapes=scratch,
            compiler_params=pltpu.CompilerParams(
                collective_id=cid, has_side_effects=True, vmem_limit_bytes=40 * 1024 * 1024
            ),
            name="tree_attention_%d" % reach,
        )

    seg = jnp.arange(parent.shape[0], dtype=jnp.int32)
    distant = jnp.any((parent > 0) & ((seg >> 2) - (parent >> 2) > 1))
    att, sc, dq, dk, dv = lax.cond(
        distant, call(ZS - 1, 1), call(1, 0),
        queries, keys, values, out_grad, reward_weight.reshape(NH, HEAD), parent, step_ends, target.T,
    )
    return pl.pallas_call(
        hand_on,
        out_shape=(wide, wide, slim, slim, jax.ShapeDtypeStruct((1, 4), F32)),
        in_specs=[hbm] * 5,
        out_specs=(hbm,) * 5,
        scratch_shapes=[pltpu.SemaphoreType.DMA((11,))],
        name="hand_on",
    )(att, dq, dk, dv, sc)


def whole(*args):
    att, dq, dk, dv, sc = local(*args)
    return att, sc, dq, dk, dv


def solution(mesh):
    both = P("seg", "head")
    return jax.shard_map(
        whole,
        mesh=mesh,
        in_specs=(both, both, both, both, P("head"), P(), P("seg", None), P()),
        out_specs=(both, P("seg", None), both, both, both),
        check_vma=False,
    )
```

```python
import functools
import math

import jax
import jax.numpy as jnp
from jax import lax
from jax.experimental import pallas as pl
from jax.experimental.pallas import tpu as pltpu
from jax.sharding import PartitionSpec as P

HEAD = 128
ROWS = 512
NH = 8
COLS = 4
ZS = 8
QUART = ROWS // COLS
HALF = ROWS // 2
SCALE = 1.0 / math.sqrt(HEAD)
C2 = SCALE * math.log2(math.e)
BF = jnp.bfloat16
F32 = jnp.float32
NEG = float("-inf")
MESH = pl.DeviceIdType.MESH
OWN, ROOT, PAR = 0, 1, 2


def nn(a, b):
    return jnp.dot(a, b, preferred_element_type=F32)


def nt(a, b):
    return lax.dot_general(a, b, (((1,), (1,)), ((), ())), preferred_element_type=F32)


def hot(cond):
    return jnp.where(cond, 1.0, 0.0).astype(F32)


def tn(a, b):
    return lax.dot_general(a, b, (((0,), (0,)), ((), ())), preferred_element_type=F32)


def exact(a, m):
    hi = a.astype(BF).astype(F32)
    mid = (a - hi).astype(BF).astype(F32)
    low = a - hi - mid
    parts = jnp.concatenate([hi, mid, low, jnp.zeros((8, HEAD), F32)], axis=0).astype(BF)
    r = nn(parts, m)
    return (r[16:24] + r[8:16]) + r[0:8]


def tree_matrices(par_ref):
    segs = COLS * ZS
    lane = lax.broadcasted_iota(jnp.int32, (HEAD, HEAD), 1)
    sub = lax.broadcasted_iota(jnp.int32, (HEAD, HEAD), 0)
    prow = jnp.full((1, HEAD), -2.0, F32)
    for s in range(segs):
        prow = jnp.where(lane[0:1] == s, par_ref[s].astype(F32), prow)
    prow = prow + jnp.zeros((HEAD, HEAD), F32)
    inside = (lane < segs) & (sub < segs)
    sib = jnp.where(inside & (prow == prow.T), 1.0, 0.0)
    up = jnp.where(inside & (prow == sub.astype(F32)), 1.0, 0.0)
    cnt = jnp.maximum(jnp.sum(sib, axis=0, keepdims=True), 1.0)
    return sib, up, up.T, cnt


def standardize(rew, tgt, sib, up, down, cnt):
    row = lax.broadcasted_iota(jnp.int32, (8, HEAD), 0)
    used = row < 4
    before = exact(rew, up)
    shifted = jnp.concatenate([before[3:4], rew[0:7]], axis=0)
    margin = jnp.where(used, rew - shifted, 0.0)
    mean = exact(margin, sib) / cnt
    cen = margin - mean
    var = exact(cen * cen, sib) / cnt
    floor = jnp.maximum(var, 0.25)
    inv = lax.rsqrt(floor)
    scores = cen * inv
    slope = jnp.where(var > 0.25, 1.0, jnp.where(var == 0.25, 0.5, 0.0))
    dvar = tgt * cen * (-0.5) * inv / floor * slope
    dcen = tgt * inv + 2.0 * cen * exact(dvar / cnt, sib)
    dmar = jnp.where(used, dcen - exact(dcen / cnt, sib), 0.0)
    back = exact(dmar, down)
    later = jnp.concatenate([dmar[1:8], dmar[0:1]], axis=0)
    later = jnp.where(row < 3, later, jnp.where(row == 3, back[0:1], 0.0))
    return scores, dmar - later


def kernel(
    reach, q_hbm, k_hbm, v_hbm, g_hbm, w_ref, par_ref, ends_ref, tgt_ref,
    att_hbm, sc_ref, dq_hbm, dk_hbm, dv_hbm,
    q_ref, g_ref, att_ref, dq_ref, dk_ref, dv_ref,
    ko, vo, kr, vr, kp, vp, vt, kt, pbuf, oacc, mrun, lrun, mblk, got, att, dl, fs, dka, dva,
    row0, row1, ep0, ep1, zb0, zb1, rq0, rq1, ps0, ps1, hrx, rrow, rpart, rall, rsend, keep, tgtp,
    pst, qst, gst, ost, wrep, pick, dqst, sibs, ups, downs, cnts,
    grs0, grs1, gps0, gps1, grx0, grx1, gpx0, gpx1, cp0, cp1, cb0, cb1,
    rrs0, rrs1, rrx0, rrx1, rsq0, rsq1, fs0, fs1, frx0, frx1,
    intx, inrx, pc0, pc1, ssem, rsem, lsem,
):
    kvo, kvr, kvp = (ko, vo), (kr, vr), (kp, vp)
    rowbuf, epart, zbuf, rootq, psend = (row0, row1), (ep0, ep1), (zb0, zb1), (rq0, rq1), (ps0, ps1)
    grs, gps, grx, gpx = (grs0, grs1), (gps0, gps1), (grx0, grx1), (gpx0, gpx1)
    cpart, cbuf, rrs, rrx = (cp0, cp1), (cb0, cb1), (rrs0, rrs1), (rrx0, rrx1)
    rsumq, fsend, frx = (rsq0, rsq1), (fs0, fs1), (frx0, frx1)
    me = lax.axis_index("seg")
    hd = lax.axis_index("head")
    z = me // COLS
    x = me % COLS
    xs = [(x + d) % COLS for d in range(COLS)]
    xdev = [z * COLS + c for c in xs]
    zdev = [((z + d) % ZS) * COLS + x for d in range(ZS)]
    count = [0]
    sent = []

    def ids(n):
        count[0] += n
        return count[0] - n

    def seg_copy(src, dst, i, seg, j=None):
        return pltpu.make_async_remote_copy(
            src_ref=src, dst_ref=dst, send_sem=ssem.at[i], recv_sem=rsem.at[i if j is None else j],
            device_id=(seg, hd), device_id_type=MESH,
        )

    def head_copy(src, dst, i, head):
        return pltpu.make_async_remote_copy(
            src_ref=src, dst_ref=dst, send_sem=ssem.at[i], recv_sem=rsem.at[i],
            device_id=(me, head), device_id_type=MESH,
        )

    def across(src, dst):
        base = ids(COLS - 1)
        out = []
        for d in (2, 1, 3):
            c = seg_copy(src(d), dst, base + d - 1, xdev[d])
            c.start()
            out.append(c)
        sent.extend(out)
        return out

    def arrive(copies):
        for c in copies:
            c.wait_recv()

    def hs(h):
        return pl.ds(pl.multiple_of(h * HEAD, HEAD), HEAD)

    def quarter(c):
        return pl.ds(pl.multiple_of(c * QUART, QUART), QUART)

    def loop(lo, hi, fn, many=2, rest=0):
        if reach > 1:
            if rest == 1:
                return
            hi, many = (NH if rest == 2 else hi), 1

        def step(h, carry):
            fn(h)
            return carry

        n = hi - lo
        lax.fori_loop(lo, hi, step, 0, unroll=many if n % many == 0 else 2 if n % 2 == 0 and many > 1 else 1)

    loads = [
        pltpu.make_async_copy(k_hbm, ko, lsem.at[0]),
        pltpu.make_async_copy(v_hbm, vo, lsem.at[1]),
        pltpu.make_async_copy(q_hbm, q_ref, lsem.at[2]),
        pltpu.make_async_copy(g_hbm, g_ref, lsem.at[3]),
    ]
    for c in loads:
        c.start()
    barrier = pltpu.get_barrier_semaphore()
    for d in range(1, COLS):
        pl.semaphore_signal(barrier, inc=1, device_id=(xdev[d], hd), device_id_type=MESH)
    for d in range(1, ZS):
        pl.semaphore_signal(barrier, inc=1, device_id=(zdev[d], hd), device_id_type=MESH)
    for d in range(1, NH):
        pl.semaphore_signal(barrier, inc=1, device_id=(me, (hd + d) % NH), device_id_type=MESH)
    lane = lax.broadcasted_iota(jnp.int32, (16, ROWS), 1)
    sub = lax.broadcasted_iota(jnp.int32, (16, ROWS), 0)
    ends = [ends_ref[0, t] for t in range(4)]
    hits = jnp.zeros((16, ROWS), F32)
    lim = jnp.zeros((8, ROWS), jnp.int32)
    kept = jnp.ones((1, ROWS), F32)
    for t in range(4):
        hits = jnp.where((sub == t) & (lane == ends[t]), 1.0, hits)
        lim = jnp.where(sub[0:8] == t, ends[t], lim)
        kept = jnp.where(lane[0:1] == ends[t], 0.0, kept)
    pick[...] = hits.astype(BF)
    keep[...] = kept
    for h in range(NH):
        wrep[8 * h:8 * h + 8, :] = w_ref[h:h + 1, :] + jnp.zeros((8, HEAD), F32)
    tgtp[...] = jnp.zeros((8, HEAD), F32)
    tgtp[0:4, 0:COLS * ZS] = tgt_ref[...]
    pl.semaphore_wait(barrier, COLS - 1 + ZS - 1 + NH - 1)

    given = (k_hbm, v_hbm)
    first = [across(lambda d: given[p].at[quarter(xs[d]), :], rowbuf[p].at[x]) for p in (0, 1)]
    for p in (0, 1):
        loads[p].wait()
        rowbuf[p][x] = kvo[p][quarter(x), :]

    lowest = lax.broadcasted_iota(jnp.int32, (HALF, HALF), 0)
    diag = lowest <= lax.broadcasted_iota(jnp.int32, (HALF, HALF), 1)

    def flip(b, kv):
        kt[b] = kv[0][...].T
        vt[b, 0:HEAD, :] = kv[1][...].T
        vt[b, HEAD:, :] = jnp.ones((16, ROWS), BF)

    def own_fwd(h):
        q = q_ref[:, hs(h)]
        qa, qb = q[0:HALF], q[HALF:]
        ka, kb = ko[0:HALF], ko[HALF:]
        s1 = jnp.where(diag, nt(ka, qa), NEG)
        s2 = nt(ka, qb)
        s3 = jnp.where(diag, nt(kb, qb), NEG)
        m1 = jnp.max(s1, axis=0, keepdims=True)
        m2 = jnp.maximum(jnp.max(s2, axis=0, keepdims=True), jnp.max(s3, axis=0, keepdims=True))
        p1 = jnp.exp2((s1 - m1) * C2).astype(BF)
        p2 = jnp.exp2((s2 - m2) * C2).astype(BF)
        p3 = jnp.exp2((s3 - m2) * C2).astype(BF)
        pbuf[OWN, h, 0:HALF, 0:HALF] = p1
        pbuf[OWN, h, 0:HALF, HALF:] = p2
        pbuf[OWN, h, HALF:, HALF:] = p3
        o1 = nn(vt[OWN, :, 0:HALF], p1)
        o2 = nn(vt[OWN, :, 0:HALF], p2) + nn(vt[OWN, :, HALF:], p3)
        oacc[h, :, 0:HALF] = o1[0:HEAD]
        oacc[h, :, HALF:] = o2[0:HEAD]
        lrun[h, :, 0:HALF] = o1[HEAD:HEAD + 1]
        lrun[h, :, HALF:] = o2[HEAD:HEAD + 1]
        mrun[h, :, 0:HALF] = m1
        mrun[h, :, HALF:] = m2
        mblk[OWN, h, :, 0:HALF] = m1
        mblk[OWN, h, :, HALF:] = m2

    my_par = par_ref[me]
    bias = {
        ROOT: jnp.where(my_par >= 0, 0.0, NEG).astype(F32),
        PAR: jnp.where(my_par > 0, 0.0, NEG).astype(F32),
    }

    def far_fwd(b, kv):
        def run(h):
            s = nt(kv[0][...], q_ref[:, hs(h)])
            m = jnp.max(s, axis=0, keepdims=True)
            p = jnp.exp2((s - m) * C2).astype(BF)
            pbuf[b, h] = p
            o = nn(vt[b], p)
            top = m + bias[b]
            old = mrun[h]
            new = jnp.maximum(old, top)
            a = jnp.exp2((old - new) * C2)
            e = jnp.exp2((top - new) * C2)
            oacc[h] = oacc[h] * a + o[0:HEAD] * e
            lrun[h] = lrun[h] * a + o[HEAD:HEAD + 1] * e
            mrun[h] = new
            mblk[b, h] = top
        return run

    flip(OWN, kvo)
    loads[2].wait()
    loop(0, 4, own_fwd, 2, 2)

    rid = ids(2 * (ZS - 1))

    def root_out(d, p):
        i = rid + p * (ZS - 1)
        return seg_copy(rootq[p], rootq[p], i + d - 1, zdev[d], i)

    last = jnp.int32(0)
    for t in range(COLS):
        last = jnp.where(par_ref[z * COLS + t] == 0, t, last)
    near_first = sorted(range(1, reach + 1), key=lambda d: -min(d, ZS - d))
    carried = [[], []]
    for p in (0, 1):
        arrive(first[p])

        epart[p][...] = rowbuf[p][last]
        base = ids(reach)
        for d in near_first:
            c = seg_copy(epart[p], zbuf[p].at[d - 1], base + d - 1, zdev[d])
            c.start()
            carried[p].append(c)
        sent += carried[p]
        @pl.when(z == 0)
        def _():
            rootq[p][...] = rowbuf[p][0]
            for d in (4, 3, 5, 2, 6, 1, 7):
                root_out(d, p).start()

        for t in range(COLS):
            zbuf[p][reach + t] = rowbuf[p][t]
    loop(4, 8, own_fwd, 2, 1)

    def spread(r):
        return jnp.concatenate([r[:, h * HEAD:(h + 1) * HEAD] for h in range(NH)], axis=0)

    qst[...] = spread(nn(pick[...], q_ref[...])[0:8]).astype(BF)
    seen = jnp.concatenate([lane[0:8] <= lim] * NH, axis=0)
    pst[OWN] = jnp.where(seen, nt(qst[...], ko[...]), NEG)

    def place(c):
        p = jnp.maximum(par_ref[z * COLS + c], 0)
        back = jnp.clip(z - p // COLS - 1, 0, reach - 1)
        return jnp.where(p // COLS == z, reach + p % COLS, back)

    third = []
    for p in (0, 1):
        arrive(carried[p])
        for d in range(1, COLS):
            psend[p][d - 1] = zbuf[p][place(xs[d])]
        third.append(across(lambda d: psend[p].at[d - 1], kvp[p].at[quarter(x), :]))
        kvp[p][quarter(x), :] = zbuf[p][place(x)]
    loads[3].wait()

    def turn(h):
        got[h] = g_ref[:, hs(h)].T

    loop(0, 8, turn, 4)
    gst[...] = spread(nn(pick[...], g_ref[...])[0:8]).astype(BF)
    sib, up, down, cnt = tree_matrices(par_ref)
    sibs[...] = sib.astype(BF)
    ups[...] = up.astype(BF)
    downs[...] = down.astype(BF)
    cnts[...] = cnt
    fourth = []
    for p in (0, 1):
        @pl.when(z != 0)
        def _():
            root_out(1, p).wait_recv()

        fourth.append(across(lambda d: rootq[p], kvr[p].at[quarter(x), :]))
        kvr[p][quarter(x), :] = rootq[p][...]
    arrive(third[0])
    pst[PAR] = nt(qst[...], kp[...]) + bias[PAR]
    arrive(third[1])
    flip(PAR, kvp)
    loop(0, 8, far_fwd(PAR, kvp), 4)
    arrive(fourth[0])
    pst[ROOT] = nt(qst[...], kr[...]) + bias[ROOT]
    arrive(fourth[1])

    m = jnp.maximum(
        jnp.max(pst[OWN], axis=1, keepdims=True),
        jnp.maximum(jnp.max(pst[ROOT], axis=1, keepdims=True), jnp.max(pst[PAR], axis=1, keepdims=True)),
    )
    total = jnp.zeros((8 * NH, 1), F32)
    for b in (OWN, ROOT, PAR):
        p = jnp.exp2((pst[b] - m) * C2)
        total = total + jnp.sum(p, axis=1, keepdims=True)
        pst[b] = p
    inv = 1.0 / total
    out = jnp.zeros((8 * NH, HEAD), F32)
    for b, kv in ((OWN, kvo), (ROOT, kvr), (PAR, kvp)):
        p = pst[b] * inv
        pst[b] = p
        out = out + nn(p.astype(BF), kv[1][...])
    out = out.astype(BF).astype(F32)
    ost[...] = out

    def pack(c):
        return [
            qst[...], gst[...], out.astype(BF),
            pst[ROOT, :, quarter(c)].astype(BF), pst[PAR, :, quarter(c)].astype(BF),
        ]

    for i, v in enumerate(pack(x)):
        inrx[x, i] = v
    for d in range(1, COLS):
        for i, v in enumerate(pack(xs[d])):
            intx[d - 1, i] = v
    terms = jnp.sum(out * wrep[...], axis=1, keepdims=True)
    part = jnp.zeros((8, 1), F32)
    for h in range(NH):
        part = part + terms[8 * h:8 * h + 8]
    mine = lax.broadcasted_iota(jnp.int32, (8, HEAD), 1) == me
    tile = jnp.where(mine, part, 0.0)
    rsend[...] = tile
    hrx[hd] = tile
    base = ids(NH - 1)
    heads = []
    for d in range(1, NH):
        c = head_copy(rsend, hrx.at[hd], base + d - 1, (hd + d) % NH)
        c.start()
        heads.append(c)
    sent += heads
    infos = across(lambda d: intx.at[d - 1], inrx.at[x])

    flip(ROOT, kvr)
    loop(0, 4, far_fwd(ROOT, kvr), 4, 2)
    loop(4, 6, far_fwd(ROOT, kvr), 4, 1)
    arrive(heads)
    total = hrx[0]
    for i in range(1, NH):
        total = total + hrx[i]
    rrow[x] = total
    rows = across(lambda d: rrow.at[x], rrow.at[x])
    loop(6, 8, far_fwd(ROOT, kvr), 4, 1)

    def finish(h):
        inv = 1.0 / lrun[h]
        a = (oacc[h] * inv).astype(BF)
        att[h] = a
        dl[h] = jnp.sum(got[h].astype(F32) * a.astype(F32), axis=0, keepdims=True)
        inv = inv * keep[...]
        for b in range(3):
            fs[b, h] = jnp.exp2((mblk[b, h] - mrun[h]) * C2) * inv

    def far_bwd(b, kv, start):
        def run(h):
            if start:
                finish(h)
            f = fs[b, h]
            gp = (got[h].astype(F32) * f).astype(BF)
            p = pbuf[b, h]
            dp = nn(kv[1][...], gp)
            ds = (p.astype(F32) * (dp - dl[h] * f)).astype(BF)
            pbuf[b, h] = ds
            dka[b] += nn(ds, q_ref[:, hs(h)])
            dva[b] += nn(p, gp.T)
        return run

    def own_bwd(h):
        f = fs[OWN, h]
        gp = (got[h].astype(F32) * f).astype(BF)
        gr = gp.T
        df = dl[h] * f
        q = q_ref[:, hs(h)]
        p1 = pbuf[OWN, h, 0:HALF, :]
        p3 = pbuf[OWN, h, HALF:, HALF:]
        d1 = (p1.astype(F32) * (nn(vo[0:HALF], gp) - df)).astype(BF)
        d3 = (p3.astype(F32) * (nn(vo[HALF:], gp[:, HALF:]) - df[:, HALF:])).astype(BF)
        dka[OWN, 0:HALF] += nn(d1, q)
        dka[OWN, HALF:] += nn(d3, q[HALF:])
        dva[OWN, 0:HALF] += nn(p1, gr)
        dva[OWN, HALF:] += nn(p3, gr[HALF:])
        far = nn(kt[ROOT], pbuf[ROOT, h]) + nn(kt[PAR], pbuf[PAR, h])
        dq = far + nn(kt[OWN, :, 0:HALF], d1)
        dq_ref[0:HALF, hs(h)] = (dq[:, 0:HALF] * SCALE).astype(BF).T
        dqb = dq[:, HALF:] + nn(kt[OWN, :, HALF:], d3)
        dq_ref[HALF:, hs(h)] = (dqb * SCALE).astype(BF).T
        att_ref[:, hs(h)] = att[h].T

    dka[...] = jnp.zeros((3, ROWS, HEAD), F32)
    dva[...] = jnp.zeros((3, ROWS, HEAD), F32)
    loop(0, 4, far_bwd(ROOT, kvr, True), 4, 2)
    arrive(rows)
    total = rrow[0]
    for t in range(1, COLS):
        total = total + rrow[t]
    rpart[...] = total
    base = ids(ZS - 1)
    along = []
    for d in (4, 3, 5, 2, 6, 1, 7):
        c = seg_copy(rpart, rall.at[z], base + d - 1, zdev[d])
        c.start()
        along.append(c)
    sent += along
    rall[z] = total
    loop(4, 8, far_bwd(ROOT, kvr, True), 4, 1)

    def scatter(send, take, b):
        out = []
        for p in (0, 1):
            send[p][...] = (dka[b] * SCALE).astype(BF) if p == 0 else dva[b].astype(BF)
            out.append(across(lambda d: send[p].at[quarter(xs[d]), :], take[p].at[x]))
            take[p][x] = send[p][quarter(x), :]
        return out

    roots = scatter(grs, grx, ROOT)
    loop(0, 8, far_bwd(PAR, kvp, False), 4)
    pars = scatter(gps, gpx, PAR)
    arrive(along)
    rew = rall[0]
    for i in range(1, ZS):
        rew = rew + rall[i]
    scores, dr = standardize(rew, tgtp[...], sibs[...], ups[...], downs[...], cnts[...])

    def step_grad(seg, g, o):
        here = lax.broadcasted_iota(jnp.int32, (8, HEAD), 1) == seg
        own = jnp.sum(jnp.where(here, dr, 0.0), axis=1, keepdims=True)
        own = jnp.where(lax.broadcasted_iota(jnp.int32, (8, 1), 0) < 4, own, 0.0)
        gs = (g.astype(F32) + jnp.concatenate([own] * NH, axis=0) * wrep[...]).astype(BF)
        return gs, jnp.sum(gs.astype(F32) * o.astype(F32), axis=1, keepdims=True)

    def share(p, v, gs, delta, q):
        ds = (p.astype(F32) * (nt(gs, v) - delta)).astype(BF)
        return tn(ds, q) * SCALE, tn(p, gs)

    arrive(infos)
    grads = [step_grad(z * COLS + t, inrx[t, 1], inrx[t, 2]) for t in range(COLS)]
    rootk, rootv = share(
        jnp.concatenate([inrx[t, 3] for t in range(COLS)], axis=0), rootq[1][...],
        jnp.concatenate([gs for gs, _ in grads], axis=0),
        jnp.concatenate([delta for _, delta in grads], axis=0),
        jnp.concatenate([inrx[t, 0] for t in range(COLS)], axis=0),
    )
    rootc = (rootk, rootv)
    sbase = ids(2)
    rbase = ids(2 * (ZS - 1))

    def root_sum(p, slot, i):
        return seg_copy(rrs[p], rrx[p].at[slot], sbase + p, x, rbase + p * (ZS - 1) + i - 1)

    for p in (0, 1):
        arrive(roots[p])
        rsum = grx[p][0].astype(F32)
        for t in range(1, COLS):
            rsum = rsum + grx[p][t].astype(F32)
        rsum = rsum + rootc[p]
        rrs[p][...] = rsum.astype(BF)
        rsumq[p][...] = jnp.zeros((QUART, HEAD), BF)

        @pl.when(z != 0)
        def _():
            root_sum(p, z, z).start()

    loop(0, 2, own_bwd, 2, 1)
    for t in range(COLS):
        gs, delta = grads[t]
        pk, pv = share(inrx[t, 4], zbuf[1][place(t)], gs, delta, inrx[t, 0])
        pc0[t] = pk
        pc1[t] = pv
    parc = (pc0, pc1)
    row_par = [par_ref[z * COLS + t] for t in range(COLS)]
    carried = [[], []]
    for p in (0, 1):
        arrive(pars[p])
        carry = jnp.zeros((QUART, HEAD), F32)
        for t in range(COLS):
            far = (row_par[t] > 0) & (row_par[t] < z * COLS)
            gpc = gpx[p][t].astype(F32) + parc[p][t]
            parc[p][t] = gpc
            carry = carry + gpc * hot(far)
        cpart[p][...] = carry.astype(BF)
        base = ids(reach)
        for d in near_first:
            c = seg_copy(cpart[p], cbuf[p].at[d - 1], base + d - 1, zdev[ZS - d])
            c.start()
            carried[p].append(c)
        sent += carried[p]
    loop(2 if reach == 1 else 0, 8, own_bwd)

    gs, delta = step_grad(me, gst[...], ost[...])
    dqs = jnp.zeros((8 * NH, HEAD), F32)
    for b, kv in ((ROOT, kvr), (PAR, kvp), (OWN, kvo)):
        p = pst[b]
        ds = (p * (nt(gs, kv[1][...]) - delta)).astype(BF)
        dqs = dqs + nn(ds, kv[0][...])
        if b == OWN:
            dka[OWN] += tn(ds, qst[...])
            dva[OWN] += tn(p.astype(BF), gs)
    for h in range(NH):
        rows16 = jnp.concatenate([dqs[8 * h:8 * h + 8], jnp.zeros((8, HEAD), F32)], axis=0)
        dqst[h] = (rows16 * SCALE).astype(BF)

    def step_dq(h):
        add = tn(pick[...], dqst[h])
        dq_ref[:, hs(h)] = (dq_ref[:, hs(h)].astype(F32) + add).astype(BF)

    loop(0, 8, step_dq, 4)
    own_score = jnp.sum(jnp.where(mine, scores, 0.0), axis=1, keepdims=True)
    at = lax.broadcasted_iota(jnp.int32, (8, HEAD), 1)
    shown = jnp.zeros((8, HEAD), F32)
    for t in range(4):
        shown = jnp.where(at == t, own_score[t:t + 1, :], shown)
    sc_ref[...] = shown[0:1, 0:4]
    stores = [
        pltpu.make_async_copy(att_ref, att_hbm, lsem.at[0]),
        pltpu.make_async_copy(dq_ref, dq_hbm, lsem.at[1]),
    ]
    stores[0].start()
    stores[1].start()

    def incoming(c, p):
        seg = z * COLS + c
        acc = rsumq[p][...].astype(F32) * hot(seg == 0)
        for t in range(COLS):
            acc = acc + parc[p][t] * hot((row_par[t] > 0) & (row_par[t] == seg))
        for d in range(1, reach + 1):
            par = par_ref[((z + d) % ZS) * COLS]
            acc = acc + cbuf[p][d - 1].astype(F32) * hot((par > 0) & (par == seg) & (z + d < ZS))
        return acc.astype(BF)

    final = []
    for p in (0, 1):
        arrive(carried[p])

        @pl.when(z == 0)
        def _():
            acc = rrs[p][...].astype(F32)
            for d in range(1, ZS):
                root_sum(p, d, d).wait_recv()
                acc = acc + rrx[p][d].astype(F32)
            rsumq[p][...] = acc.astype(BF)

        for d in range(1, COLS):
            fsend[p][d - 1] = incoming(xs[d], p)
        final.append(across(lambda d: fsend[p].at[d - 1], frx[p].at[quarter(x), :]))
        frx[p][quarter(x), :] = incoming(x, p)
    arrive(final[0])
    dk_ref[...] = (dka[OWN] * SCALE + frx[0][...].astype(F32)).astype(BF)
    stores.append(pltpu.make_async_copy(dk_ref, dk_hbm, lsem.at[2]))
    stores[2].start()
    arrive(final[1])
    dv_ref[...] = (dva[OWN] + frx[1][...].astype(F32)).astype(BF)
    stores.append(pltpu.make_async_copy(dv_ref, dv_hbm, lsem.at[3]))
    stores[3].start()

    for c in sent:
        c.wait_send()

    @pl.when(z == 0)
    def _():
        for p in (0, 1):
            for d in range(1, ZS):
                root_out(d, p).wait_send()

    @pl.when(z != 0)
    def _():
        for p in (0, 1):
            root_sum(p, z, z).wait_send()

    for c in stores:
        c.wait()


def hand_on(a_in, q_in, k_in, v_in, s_in, a_out, q_out, k_out, v_out, s_out, sem):
    copies = []
    for src, dst, parts in ((a_in, a_out, 4), (q_in, q_out, 4), (k_in, k_out, 1), (v_in, v_out, 1)):
        n = ROWS // parts
        for i in range(parts):
            rows = pl.ds(i * n, n)
            copies.append(pltpu.make_async_copy(src.at[rows, :], dst.at[rows, :], sem.at[len(copies)]))
    copies.append(pltpu.make_async_copy(s_in, s_out, sem.at[len(copies)]))
    for c in copies:
        c.start()
    for c in copies:
        c.wait()


def local(queries, keys, values, out_grad, reward_weight, parent, step_ends, target):
    vmem = pl.BlockSpec(memory_space=pltpu.VMEM)
    smem = pl.BlockSpec(memory_space=pltpu.SMEM)
    hbm = pl.BlockSpec(memory_space=pl.ANY)
    wide = jax.ShapeDtypeStruct((ROWS, NH * HEAD), BF)
    slim = jax.ShapeDtypeStruct((ROWS, HEAD), BF)
    V = pltpu.VMEM
    blk = (QUART, HEAD)
    full = (ROWS, HEAD)
    stat = (NH, 1, ROWS)
    tile = (8, HEAD)
    steps = (8 * NH, HEAD)

    def two(shape):
        return (V(shape, BF), V(shape, BF))

    def call(reach, cid):
        scratch = [
            V((ROWS, NH * HEAD), BF), V((ROWS, NH * HEAD), BF), V((ROWS, NH * HEAD), BF),
            V((ROWS, NH * HEAD), BF), V((ROWS, HEAD), BF), V((ROWS, HEAD), BF),
            *two(full) * 3,
            V((3, HEAD + 16, ROWS), BF), V((3, HEAD, ROWS), BF),
            V((3, NH, ROWS, ROWS), BF),
            V((NH, HEAD, ROWS), F32), V(stat, F32), V(stat, F32), V((3,) + stat, F32),
            V((NH, HEAD, ROWS), BF), V((NH, HEAD, ROWS), BF), V(stat, F32), V((3,) + stat, F32),
            V((3, ROWS, HEAD), F32), V((3, ROWS, HEAD), F32),
            *two((COLS,) + blk), *two(blk), *two((reach + COLS,) + blk), *two(blk), *two((COLS - 1,) + blk),
            V((NH,) + tile, F32), V((COLS,) + tile, F32), V(tile, F32), V((ZS,) + tile, F32), V(tile, F32),
            V((1, ROWS), F32), V(tile, F32),
            V((3, 8 * NH, ROWS), F32), V(steps, BF), V(steps, BF), V(steps, F32), V(steps, F32),
            V((16, ROWS), BF), V((NH, 16, HEAD), BF),
            V((HEAD, HEAD), BF), V((HEAD, HEAD), BF), V((HEAD, HEAD), BF), V((1, HEAD), F32),
            *two(full) * 2, *two((COLS,) + blk) * 2,
            *two(blk), *two((reach,) + blk), *two(blk), *two((ZS,) + blk), *two(blk),
            *two((COLS - 1,) + blk), *two(full),
            V((COLS - 1, 5) + steps, BF), V((COLS, 5) + steps, BF),
            V((COLS,) + blk, F32), V((COLS,) + blk, F32),
            pltpu.SemaphoreType.DMA((128,)), pltpu.SemaphoreType.DMA((128,)), pltpu.SemaphoreType.DMA((4,)),
        ]
        return pl.pallas_call(
            functools.partial(kernel, reach),
            out_shape=(wide, jax.ShapeDtypeStruct((1, 4), F32), wide, slim, slim),
            in_specs=[hbm, hbm, hbm, hbm, vmem, smem, smem, vmem],
            out_specs=(hbm, vmem, hbm, hbm, hbm),
            scratch_shapes=scratch,
            compiler_params=pltpu.CompilerParams(
                collective_id=cid, has_side_effects=True, vmem_limit_bytes=40 * 1024 * 1024
            ),
            name="tree_attention_%d" % reach,
        )

    seg = jnp.arange(parent.shape[0], dtype=jnp.int32)
    back = jnp.max(jnp.where(parent > 0, (seg >> 2) - (parent >> 2), 0))
    att, sc, dq, dk, dv = lax.switch(
        jnp.clip(back - 1, 0, 2), [call(1, 0), call(2, 1), call(ZS - 1, 2)],
        queries, keys, values, out_grad, reward_weight.reshape(NH, HEAD), parent, step_ends, target.T,
    )
    return pl.pallas_call(
        hand_on,
        out_shape=(wide, wide, slim, slim, jax.ShapeDtypeStruct((1, 4), F32)),
        in_specs=[hbm] * 5,
        out_specs=(hbm,) * 5,
        scratch_shapes=[pltpu.SemaphoreType.DMA((11,))],
        name="hand_on",
    )(att, dq, dk, dv, sc)


def whole(*args):
    att, dq, dk, dv, sc = local(*args)
    return att, sc, dq, dk, dv


def solution(mesh):
    both = P("seg", "head")
    return jax.shard_map(
        whole,
        mesh=mesh,
        in_specs=(both, both, both, both, P("head"), P(), P("seg", None), P()),
        out_specs=(both, P("seg", None), both, both, both),
        check_vma=False,
    )
```
